768 devices in a mesh: replica: 16 (over x_lo, y), expert: 48 (over x_hi, z, core).
Axes of the slice: x: 4 (x_hi: 2, x_lo: 2; x = x_hi * 2 + x_lo), y: 8, z: 12, core: 2. Of those that a mesh axis runs over, the one named last changes fastest.
Arguments:
- tokens: bfloat16 [16, 6144, 1024], P('replica', 'expert'), may hold values from -6 to 6
- expert_ids: int32 [16, 6144, 8], P('replica', 'expert'), may hold values from 0 to 95, all different within a row; in each aligned block of 64 rows (0 to 63, 64 to 127, ..., all dimensions but the last counted through in order) at most 7 rows name the same one
- hidden_grad: bfloat16 [16, 6144, 8, 384], P('replica', 'expert'), may hold values from -0.59765625 to 0.59765625
- gate_weight: bfloat16 [96, 1024, 384], P('expert'), may hold values from -0.1875 to 0.1875
- up_weight: bfloat16 [96, 1024, 384], P('expert'), may hold values from -0.1875 to 0.1875
- outer_params: float32 [384, 2048], P('expert'), may hold values from -6 to 6
- momentum: float32 [384, 2048], P('expert'), may hold values from -3 to 3
- inner_params: float32 [16, 384, 2048], P('replica', 'expert'), may hold values from -6 to 6
Outputs:
- gate_grad: bfloat16 [16, 96, 1024, 384], P('replica', 'expert')
- up_grad: bfloat16 [16, 96, 1024, 384], P('replica', 'expert')
- new_outer: float32 [384, 2048], P('expert')
- new_momentum: float32 [384, 2048], P('expert')
The draws below stay inside these ranges and needn't reach their ends.
Inputs may be any that keep to these rules, and one draw needn't show every extreme that they name: `expert_ids`: each token names 8 different experts; among the 64 tokens of one block no expert is chosen more than 7 times, a bound that some block reaches.
All inputs are finite; a program needn't handle non-finite values.
Results may differ from the reference program's by a relative error of at most 0.012.
Values may be sent and summed in bfloat16 or wider, within the bound.
A program may use at most 64 MiB of HBM per device.

```python
import math
import jax
import jax.numpy as jnp
import numpy as np
from jax import lax

D = 1024
FF = 384
TOP = 8
BLOCKS = 2
FW = 2048
EXPERTS = 96
TOK_BLK = 64
CAP = 7
TOKENS = 6144
FR = 384
N_REPLICA = 16
N_EXPERT = 48


def level_of(rng, dims, pieces, least, high):
    def one(dim, blocks):
        heights = jax.random.uniform(jax.random.fold_in(jax.random.fold_in(rng, 6), dim), (blocks,), jnp.float32, least / len(pieces), high / len(pieces))
        return jnp.repeat(jnp.exp(heights), dims[dim] // blocks).reshape((-1,) + (1,) * (len(dims) - dim - 1))

    loudness = one(*pieces[0])
    for cut in pieces[1:]:
        loudness = loudness * one(*cut)
    return loudness


def deal_out(rng, own, number, rows, number_of, top, limit, skew):
    sequence = jax.random.permutation(rng, number_of)
    crowded, ordinary = shares(number_of, rows * top, limit, skew, True), shares(number_of, rows * top, limit, skew, False)
    places = jnp.arange(number_of)

    def named(sizes, rotation):
        used = int((sizes > 0).sum())
        fixed = max(1, used // 4)
        shifted = fixed + (places - fixed + rotation * (used - fixed)) % max(1, number_of - fixed)
        return jnp.zeros((number_of,), jnp.int32).at[sequence[jnp.where(places < fixed, places, shifted)]].set(jnp.asarray(sizes, jnp.int32))

    sizes = jnp.where(number % 4 == 0, named(crowded, number // 4), named(ordinary, number - number // 4 - 1))
    mixed = jax.random.permutation(jax.random.fold_in(own, 3), number_of)
    giver, sink = mixed[0:number_of // 2 * 2:2], mixed[1:number_of // 2 * 2:2]
    slack = jnp.minimum(sizes[giver] - 1, limit - sizes[sink]) // 2
    slack = jnp.where((giver == sequence[0]) | (sink == sequence[0]) | (sizes[sink] == 0), 0, jnp.maximum(slack, 0))
    shifted = jax.random.randint(jax.random.fold_in(own, 4), (number_of // 2,), 0, 1 << 20) % (slack + 1)
    sizes = sizes.at[giver].add(-shifted).at[sink].add(shifted)
    items = jnp.searchsorted(jnp.cumsum(sizes), jnp.arange(rows * top), side="right").astype(jnp.int32)
    listing = items.reshape(top, rows).T
    listing = listing[jax.random.permutation(jax.random.fold_in(own, 1), rows)]
    rotation = jax.random.randint(jax.random.fold_in(own, 2), (rows, 1), 0, top)
    return jnp.take_along_axis(listing, (jnp.arange(top)[None, :] + rotation) % top, axis=1)


def shares(number_of, total, limit, lean, full):
    loads = [(1 << 20) // math.isqrt(grade ** lean) + 1 for grade in range(1, number_of + 1)]
    largest = limit if full else min(limit, max(-(-total // number_of), total * loads[0] // sum(loads)))
    least = 1 if total - largest >= number_of - 1 else 0
    counts, rest = [largest] + [least] * (number_of - 1), total - largest - least * (number_of - 1)
    while rest > 0:
        candidates = [i for i in range(1, number_of) if counts[i] < largest] or [i for i in range(1, number_of) if counts[i] < limit]
        mass, remaining = sum([loads[i] for i in candidates]), rest
        for i in candidates:
            more = min(limit - counts[i], max(1, remaining * loads[i] // mass), rest)
            counts[i] = counts[i] + more
            rest = rest - more
    return np.array(counts)


def gaussian(key, shape, spread, limit, pieces=(), held_as=jnp.bfloat16):
    level = level_of(key, shape, pieces, -0.22, 0.18) if pieces else 1.0
    drawn = jax.random.normal(key, shape, jnp.float32) * spread * level
    return jnp.minimum(jnp.maximum(drawn, -limit), limit).astype(held_as)


def setup_inputs(seed: int = 0) -> dict:
    seeds = jax.random.split(jax.random.key(seed), 9)
    tokens = gaussian(seeds[0], (N_REPLICA, TOKENS, D), 1.0, 6.0, ((0, 16), (1, 48)))
    expert_ids_keys = jax.random.split(jax.random.fold_in(seeds[1], 1), N_REPLICA * TOKENS // TOK_BLK)
    expert_ids_turns = jax.random.permutation(jax.random.fold_in(seeds[1], 3), N_REPLICA * TOKENS // TOK_BLK)
    expert_ids = jax.vmap(lambda own, number: deal_out(jax.random.fold_in(seeds[1], 2), own, number, TOK_BLK, EXPERTS, TOP, CAP, 2))(expert_ids_keys, expert_ids_turns).reshape((N_REPLICA, TOKENS, TOP))
    hidden_grad = gaussian(seeds[2], (N_REPLICA, TOKENS, TOP, FF), 0.1, 0.59765625, ((0, 16), (1, 48)))
    gate_weight = gaussian(seeds[3], (EXPERTS, D, FF), D ** -0.5, 0.1875, ((0, 48),))
    up_weight = gaussian(seeds[4], (EXPERTS, D, FF), D ** -0.5, 0.1875, ((0, 48),))
    outer_params = gaussian(seeds[5], (FR, FW), 1.0, 6.0, ((0, 48),), jnp.float32)
    momentum = gaussian(seeds[6], (FR, FW), 0.5, 3.0, ((0, 48),), jnp.float32)
    inner_params = gaussian(seeds[7], (N_REPLICA, FR, FW), 1.0, 6.0, ((0, 16), (1, 48)), jnp.float32)
    return {"tokens": tokens, "expert_ids": expert_ids, "hidden_grad": hidden_grad, "gate_weight": gate_weight, "up_weight": up_weight, "outer_params": outer_params, "momentum": momentum, "inner_params": inner_params}


def slot_ranks(ids, count):
    hits = (ids[:, :, None] == jnp.arange(count, dtype=jnp.int32)[None, None, :]).astype(jnp.int32)
    chosen = jnp.sum(hits, axis=1)
    before = jnp.cumsum(chosen, axis=0) - chosen
    return jnp.sum(hits * before[:, None, :], axis=2).astype(jnp.int32)


def build_slots(block_tokens, block_ids, block_grad):
    slot = slot_ranks(block_ids, EXPERTS)
    flat = (block_ids * CAP + slot).reshape(-1)
    width = block_tokens.shape[1]
    repeated = jnp.broadcast_to(block_tokens[:, None, :], (block_tokens.shape[0], TOP, width)).reshape(-1, width)
    slots_x = jnp.zeros((EXPERTS * CAP, width), jnp.bfloat16).at[flat].set(repeated)
    slots_h = jnp.zeros((EXPERTS * CAP, FF), jnp.bfloat16).at[flat].set(block_grad.reshape(-1, FF))
    return slots_x.reshape(EXPERTS, CAP, width), slots_h.reshape(EXPERTS, CAP, FF)


def group_grads(tokens_g, ids_g, grad_g, gate_weight, up_weight):
    count = N_EXPERT * BLOCKS
    blocks_x, blocks_h = jax.vmap(build_slots)(tokens_g.reshape(count, TOK_BLK, D), ids_g.reshape(count, TOK_BLK, TOP), grad_g.reshape(count, TOK_BLK, TOP, FF))
    rows_x = jnp.transpose(blocks_x, (1, 0, 2, 3)).reshape(EXPERTS, count * CAP, D).astype(jnp.float32)
    rows_h = jnp.transpose(blocks_h, (1, 0, 2, 3)).reshape(EXPERTS, count * CAP, FF).astype(jnp.float32)
    gate = jnp.einsum('erd,edf->erf', rows_x, gate_weight.astype(jnp.float32))
    upval = jnp.einsum('erd,edf->erf', rows_x, up_weight.astype(jnp.float32))
    sig = jax.nn.sigmoid(gate)
    gate_d = (rows_h * upval * sig * (1.0 + gate * (1.0 - sig))).astype(jnp.bfloat16).astype(jnp.float32)
    up_d = (rows_h * gate * sig).astype(jnp.bfloat16).astype(jnp.float32)
    gate_grad = jnp.einsum('erd,erf->edf', rows_x, gate_d).astype(jnp.bfloat16)
    up_grad = jnp.einsum('erd,erf->edf', rows_x, up_d).astype(jnp.bfloat16)
    return gate_grad, up_grad


def reference(tokens, expert_ids, hidden_grad, gate_weight, up_weight, outer_params, momentum, inner_params):
    def one_group(packed):
        return group_grads(packed[0], packed[1], packed[2], gate_weight, up_weight)

    gate_grad, up_grad = lax.map(one_group, (tokens, expert_ids, hidden_grad))
    delta = outer_params - jnp.sum(inner_params, axis=0) / N_REPLICA
    new_momentum = 0.9 * momentum + delta
    new_outer = outer_params - 0.7 * (delta + 0.9 * new_momentum)
    return gate_grad, up_grad, new_outer, new_momentum
```

```python
import jax
import jax.numpy as jnp
from jax import lax
from jax.experimental import pallas as pl
from jax.experimental.pallas import tpu as pltpu
from jax.sharding import PartitionSpec as P

MESH = pl.DeviceIdType.MESH
NZ = 12
NY = 8
SLOTS = 7
ROWS = 16
ARRIVAL = [0, 1, 11, 2, 10, 3, 9, 4, 8, 5, 7, 6]
POS = {o: p for p, o in enumerate(ARRIVAL)}
FAR = [6, 5, 7, 4, 8, 3, 9, 2, 10, 1, 11, 0]
LEAVE = (2, 3, 4)
F32 = jnp.float32
BF16 = jnp.bfloat16


def iota(shape, dim):
    return lax.broadcasted_iota(jnp.int32, shape, dim)


def onehot(mask):
    return jnp.where(mask, 1.0, 0.0).astype(BF16)


def dispatch_kernel(
    ids_ref, tok_h, hid_h, gate_h, up_h, inner_h,
    x_o, g_o, sum_o,
    tok, meta, xs, xr, hid, hs, hq, hr, w, gu, gd, yr, part,
    load_sem, tok_s, tok_r, meta_s, meta_r, x_s, x_r, hp_s, hp_r, hz_s, hz_r,
    y_s, y_r, l_s, l_r, own_sem, out_sem,
):
    replica = lax.axis_index("replica")
    expert = lax.axis_index("expert")
    xlo, y = replica // NY, replica % NY
    xhi, z, c = expert // (2 * NZ), (expert // 2) % NZ, expert % 2

    def at(dz=0, s=0):
        x2 = (xhi + s // 2) % 2
        c2 = (c + s % 2) % 2
        return (replica, (x2 * NZ + (z + dz) % NZ) * 2 + c2)

    def at_y(dy, dl=0):
        return (((xlo + dl) % 2) * NY + (y + dy) % NY, expert)

    loads = [
        pltpu.make_async_copy(tok_h, tok.at[0], load_sem.at[0]),
        pltpu.make_async_copy(hid_h, hid, load_sem.at[1]),
        pltpu.make_async_copy(gate_h, w.at[:, :, pl.ds(0, 384)], load_sem.at[2]),
        pltpu.make_async_copy(up_h, w.at[:, :, pl.ds(384, 384)], load_sem.at[3]),
        pltpu.make_async_copy(inner_h, yr.at[y], load_sem.at[4]),
    ]
    for load in loads:
        load.start()

    barrier = pltpu.get_barrier_semaphore()
    peers = [at(dz) for dz in range(1, NZ)] + [at(0, s) for s in (1, 2, 3)]
    peers += [at_y(dy) for dy in range(1, NY)] + [at_y(0, 1)]
    for peer in peers:
        pl.semaphore_signal(barrier, inc=1, device_id=peer, device_id_type=MESH)
    pl.semaphore_wait(barrier, len(peers))

    def remote(src, dst, send, recv, device):
        return pltpu.make_async_remote_copy(
            src_ref=src, dst_ref=dst, send_sem=send, recv_sem=recv,
            device_id=device, device_id_type=MESH,
        )

    def token_copy(step, way, half):
        sign = 1 if way == 0 else -1
        rows = pl.ds(half * 64, 64)
        dst = POS[(sign * step) % NZ]
        src = tok_h.at[rows] if step == 1 else tok.at[POS[(sign * (step - 1)) % NZ], rows]
        return remote(
            src, tok.at[dst, rows], tok_s.at[dst, half], tok_r.at[dst, half], at(-sign)
        )

    def meta_copy(step, way):
        sign = 1 if way == 0 else -1
        dst = POS[(sign * step) % NZ]
        return remote(
            meta.at[POS[(sign * (step - 1)) % NZ]], meta.at[dst],
            meta_s.at[dst], meta_r.at[dst], at(-sign),
        )

    def ways(step, half):
        return (0, 1) if step < NZ // 2 else (half,)

    sent = []

    def go(copy):
        copy.start()
        sent.append(copy)
        return copy

    ring = {}
    for half in (0, 1):
        for way in ways(1, half):
            ring[1, way, half] = go(token_copy(1, way, half))
    gathers = [
        go(remote(inner_h, yr.at[y], y_s.at[dy], y_r.at[dy], at_y(dy))) for dy in range(1, NY)
    ]

    pick = onehot(iota((128, 1024), 1) // 8 == iota((128, 1024), 0))
    spread = jnp.dot(ids_ref[...].astype(F32).astype(BF16), pick, preferred_element_type=F32)
    mine = iota((8, 1024), 1) % 8 == iota((8, 1024), 0)
    ids = jnp.sum(jnp.where(mine, spread, 0.0), axis=0, keepdims=True)
    earlier = onehot(iota((512, 512), 0) // 8 < iota((512, 512), 1) // 8)
    experts = iota((96, 512), 0).astype(F32)
    slots = []
    for block in (0, 1):
        hits = experts == ids[:, block * 512 : (block + 1) * 512]
        before = jnp.dot(onehot(hits), earlier, preferred_element_type=F32)
        slots.append(
            jnp.sum(jnp.where(hits, before, 0.0), axis=0, keepdims=True) + float(SLOTS * block)
        )
    slot = jnp.concatenate(slots, axis=1)
    chip = jnp.floor(ids * 0.25)
    far_x = jnp.where(chip >= float(NZ), 1.0, 0.0)
    inside = ids - 4.0 * chip
    core = jnp.where(inside >= 2.0, 1.0, 0.0)
    local = inside - 2.0 * core
    dz = chip - float(NZ) * far_x - z.astype(F32)
    dz = jnp.where(dz < 0.0, dz + float(NZ), dz)
    rel = jnp.where(far_x == xhi.astype(F32), 0.0, 2.0) + jnp.where(core == c.astype(F32), 0.0, 1.0)
    lane = rel * 32.0 + local * 16.0 + slot
    order = jnp.where(
        dz > 6.0, 2.0 * dz - 12.0, jnp.where(dz == 6.0, 0.0, 11.0 - 2.0 * dz)
    )
    row = order * 128.0 + lane
    token = (iota((16, 1024), 1) // 8 + 1).astype(F32)
    lines = jnp.where(iota((16, 1024), 0).astype(F32) == dz, token, 0.0).astype(BF16)
    places = onehot(iota((128, 1024), 0).astype(F32) == lane)
    meta[0] = lax.dot_general(
        lines, places, (((1,), (1,)), ((), ())), preferred_element_type=F32
    )
    metas = {}
    for way in (0, 1):
        metas[1, way] = go(meta_copy(1, way))

    loads[1].wait()
    plane = {}
    rows_of = iota((256, 1024), 0).astype(F32)
    for third in range(3):
        for pair in (2 * third, 2 * third + 1):
            take = onehot(rows_of == row - float(256 * pair))
            packed = jnp.dot(take, hid[...], preferred_element_type=F32).astype(BF16)
            for i in range(2):
                for s in range(4):
                    for e in range(2):
                        at_row = ((i * 4 + s) * 2 + e) * ROWS
                        hs[2 * pair + i, s, e] = packed[at_row : at_row + ROWS]
        part_of = pl.ds(4 * third, 4)
        for s in (1, 2, 3):
            plane[third, s] = go(
                remote(
                    hs.at[part_of, s], hq.at[part_of, s],
                    hp_s.at[third, s], hp_r.at[third, s], at(0, s),
                )
            )
        plane[third, 0] = pltpu.make_async_copy(
            hs.at[part_of, 0], hq.at[part_of, 0], hp_r.at[third, 0]
        )
        plane[third, 0].start()

    rows_sent = {}

    def pick_rows(offset):
        p = POS[offset]
        line = (-offset) % NZ
        wanted = meta[p][line : line + 1, :]
        take = onehot((iota((128, 128), 0) + 1).astype(F32) == wanted)
        rows = lax.dot_general(
            take, tok[p], (((0,), (0,)), ((), ())), preferred_element_type=F32
        ).astype(BF16)
        for s in range(4):
            for e in range(2):
                at_row = (s * 2 + e) * ROWS
                xs[p, s, e] = rows[at_row : at_row + ROWS]
        for s in (1, 2, 3):
            rows_sent[p, s] = go(
                remote(xs.at[p, s], xr.at[p, s], x_s.at[p, s], x_r.at[p, s], at(0, s))
            )
        rows_sent[p, 0] = pltpu.make_async_copy(xs.at[p, 0], xr.at[p, 0], x_r.at[p, 0])
        rows_sent[p, 0].start()

    stay = pltpu.make_async_copy(hq.at[11], hr.at[POS[0]], own_sem.at[0])
    along = {}

    def leave(third):
        plane[third, 0].wait()
        for s in (1, 2, 3):
            plane[third, s].wait_recv()
        for q in range(4 * third, 4 * third + 4):
            distance = FAR[q]
            if distance == 0:
                stay.start()
            else:
                p = POS[(-distance) % NZ]
                along[p] = go(
                    remote(hq.at[q], hr.at[p], hz_s.at[p], hz_r.at[p], at(distance))
                )

    outs = []

    def project(group):
        for p in range(4 * group, 4 * group + 4):
            rows_sent[p, 0].wait()
            for s in (1, 2, 3):
                rows_sent[p, s].wait_recv()
        for e in range(2):
            block = pl.ds(4 * group, 4)
            rows = xr[block, :, e].reshape(256, 1024)
            gu[e, group] = jnp.dot(rows, w[e], preferred_element_type=F32)
            out = pltpu.make_async_copy(
                xr.at[block, :, e], x_o.at[e, block], out_sem.at[e, group]
            )
            out.start()
            outs.append(out)

    loads[0].wait()
    pick_rows(0)
    for step in range(1, NZ // 2 + 1):
        for half in (0, 1):
            for way in ways(step, half):
                ring[step, way, half].wait_recv()
                if step < NZ // 2 and way in ways(step + 1, half):
                    ring[step + 1, way, half] = go(token_copy(step + 1, way, half))
            if half == 0:
                for way in ways(step, 0):
                    metas[step, way].wait_recv()
                    if step < NZ // 2 and way in ways(step + 1, 0):
                        metas[step + 1, way] = go(meta_copy(step + 1, way))
        for third in range(3):
            if LEAVE[third] == step:
                leave(third)
        for offset in dict.fromkeys((step, NZ - step)):
            pick_rows(offset)
        if step == 3:
            loads[4].wait()
            for gather in gathers:
                gather.wait_recv()
            total = yr[0]
            for i in range(1, NY):
                total = total + yr[i]
            part[0] = total
            swap = go(remote(part.at[0], part.at[1], l_s, l_r, at_y(0, 1)))
        if step == 4:
            loads[2].wait()
            loads[3].wait()
            project(0)
        if step == 5:
            swap.wait_recv()
            sum_o[...] = part[0] + part[1]
        if step == 6:
            project(1)
    project(2)

    stay_waited = False
    for group in (2, 1, 0):
        for p in range(4 * group, 4 * group + 4):
            if p == POS[0]:
                stay.wait()
            else:
                along[p].wait_recv()
        for e in range(2):
            cot = hr[pl.ds(4 * group, 4), :, e].reshape(256, 384).astype(F32)
            gate = gu[e, group, :, 0:384]
            up = gu[e, group, :, 384:768]
            sig = jax.nn.sigmoid(gate)
            gd[e, group, :, 0:384] = (cot * up * sig * (1.0 + gate * (1.0 - sig))).astype(BF16)
            gd[e, group, :, 384:768] = (cot * gate * sig).astype(BF16)
            out = pltpu.make_async_copy(
                gd.at[e, group], g_o.at[e, group], out_sem.at[2 + e, group]
            )
            out.start()
            outs.append(out)
    for copy in sent:
        copy.wait_send()
    for out in outs:
        out.wait()


def grad_kernel(x_ref, g_ref, sum_ref, outer_ref, mom_ref, gate_ref, up_ref, no_ref, nm_ref):
    grads = lax.dot_general(
        x_ref[0], g_ref[0], (((0,), (0,)), ((), ())), preferred_element_type=F32
    ).astype(BF16)
    gate_ref[0] = grads[:, 0:384]
    up_ref[0] = grads[:, 384:768]
    delta = outer_ref[...] - sum_ref[...] / 16.0
    momentum = 0.9 * mom_ref[...] + delta
    nm_ref[...] = momentum
    no_ref[...] = outer_ref[...] - 0.7 * (delta + 0.9 * momentum)


def local(tokens, ids, hidden, gate_weight, up_weight, outer, momentum, inner):
    any_ = pl.BlockSpec(memory_space=pl.ANY)
    vmem = pl.BlockSpec(memory_space=pltpu.VMEM)
    dma = pltpu.SemaphoreType.DMA
    x_rows, g_rows, summed = pl.pallas_call(
        dispatch_kernel,
        out_shape=(
            jax.ShapeDtypeStruct((2, NZ, 4, ROWS, 1024), BF16),
            jax.ShapeDtypeStruct((2, 3, 256, 768), BF16),
            jax.ShapeDtypeStruct((8, 2048), F32),
        ),
        in_specs=[vmem, any_, any_, any_, any_, any_],
        out_specs=(any_, any_, vmem),
        scratch_shapes=[
            pltpu.VMEM((NZ, 128, 1024), BF16),
            pltpu.VMEM((NZ, 16, 128), F32),
            pltpu.VMEM((NZ, 4, 2, ROWS, 1024), BF16),
            pltpu.VMEM((NZ, 4, 2, ROWS, 1024), BF16),
            pltpu.VMEM((1024, 384), BF16),
            pltpu.VMEM((NZ, 4, 2, ROWS, 384), BF16),
            pltpu.VMEM((NZ, 4, 2, ROWS, 384), BF16),
            pltpu.VMEM((NZ, 4, 2, ROWS, 384), BF16),
            pltpu.VMEM((2, 1024, 768), BF16),
            pltpu.VMEM((2, 3, 256, 768), F32),
            pltpu.VMEM((2, 3, 256, 768), BF16),
            pltpu.VMEM((NY, 8, 2048), F32),
            pltpu.VMEM((2, 8, 2048), F32),
            dma((5,)), dma((NZ, 2)), dma((NZ, 2)), dma((NZ,)), dma((NZ,)),
            dma((NZ, 4)), dma((NZ, 4)), dma((3, 4)), dma((3, 4)), dma((NZ,)), dma((NZ,)),
            dma((NY,)), dma((NY,)), dma, dma, dma((1,)), dma((4, 3)),
        ],
        compiler_params=pltpu.CompilerParams(
            collective_id=0, has_side_effects=True, vmem_limit_bytes=60 << 20
        ),
        cost_estimate=pl.CostEstimate(
            flops=4_000_000_000, bytes_accessed=16_000_000, transcendentals=600_000
        ),
    )(ids[0].T, tokens[0], hidden[0].reshape(1024, 384), gate_weight, up_weight, inner[0])
    x_rows = x_rows.reshape(2, 768, 1024)
    g_rows = g_rows.reshape(2, 768, 768)
    gate_grad, up_grad, new_outer, new_momentum = pl.pallas_call(
        grad_kernel,
        grid=(2, 2),
        out_shape=(
            jax.ShapeDtypeStruct((2, 1024, 384), BF16),
            jax.ShapeDtypeStruct((2, 1024, 384), BF16),
            jax.ShapeDtypeStruct((8, 2048), F32),
            jax.ShapeDtypeStruct((8, 2048), F32),
        ),
        in_specs=[
            pl.BlockSpec((1, 768, 512), lambda e, m: (e, 0, m)),
            pl.BlockSpec((1, 768, 768), lambda e, m: (e, 0, 0)),
            pl.BlockSpec((8, 2048), lambda e, m: (0, 0)),
            pl.BlockSpec((8, 2048), lambda e, m: (0, 0)),
            pl.BlockSpec((8, 2048), lambda e, m: (0, 0)),
        ],
        out_specs=(
            pl.BlockSpec((1, 512, 384), lambda e, m: (e, m, 0)),
            pl.BlockSpec((1, 512, 384), lambda e, m: (e, m, 0)),
            pl.BlockSpec((8, 2048), lambda e, m: (0, 0)),
            pl.BlockSpec((8, 2048), lambda e, m: (0, 0)),
        ),
        compiler_params=pltpu.CompilerParams(vmem_limit_bytes=60 << 20),
    )(x_rows, g_rows, summed, outer, momentum)
    return gate_grad[None], up_grad[None], new_outer, new_momentum


def solution(mesh):
    rows = P("replica", "expert", None)
    return jax.shard_map(
        local,
        mesh=mesh,
        in_specs=(
            rows,
            rows,
            P("replica", "expert", None, None),
            P("expert", None, None),
            P("expert", None, None),
            P("expert", None),
            P("expert", None),
            rows,
        ),
        out_specs=(
            P("replica", "expert", None, None),
            P("replica", "expert", None, None),
            P("expert", None),
            P("expert", None),
        ),
        check_vma=False,
    )
```

```python
import jax
import jax.numpy as jnp
from jax import lax
from jax.experimental import pallas as pl
from jax.experimental.pallas import tpu as pltpu
from jax.sharding import PartitionSpec as P

MESH = pl.DeviceIdType.MESH
NZ = 12
NY = 8
SLOTS = 7
ROWS = 16
ARRIVAL = [0, 1, 11, 2, 10, 3, 9, 4, 8, 5, 7, 6]
POS = {o: p for p, o in enumerate(ARRIVAL)}
FAR = [6, 5, 7, 4, 8, 3, 9, 2, 10, 1, 11, 0]
LEAVE = (4, 4, 5, 5, 5, 5, 5, 6, 6, 6, 6, 6)
FINISH = (2, 1, 0)
PAIR = 28
LINE = 4 * PAIR
F32 = jnp.float32
BF16 = jnp.bfloat16


def iota(shape, dim):
    return lax.broadcasted_iota(jnp.int32, shape, dim)


def onehot(mask):
    return jnp.where(mask, 1.0, 0.0).astype(BF16)


def digits(value, *weights):
    out = []
    for weight in weights:
        digit = jnp.floor((value + 0.5) * (1.0 / weight))
        value = value - digit * weight
        out.append(digit)
    return (*out, value)


def dispatch_kernel(
    ids_ref, tok_h, hid_h, gate_h, up_h, inner_h,
    x_o, g_o, some_o, sum_o,
    tok, meta, xs, xr, xt, hid, hs, hq, hz, hr, w, gu, gd, acc, some, yr, part,
    load_sem, tok_s, tok_r, meta_s, meta_r, x_s, x_r, hp_s, hp_r, hz_s, hz_r,
    y_s, y_r, l_s, l_r, out_sem,
):
    replica = lax.axis_index("replica")
    expert = lax.axis_index("expert")
    xlo, y = replica // NY, replica % NY
    xhi, z, c = expert // (2 * NZ), (expert // 2) % NZ, expert % 2

    def at(dz=0, s=0):
        x2 = (xhi + s // 2) % 2
        c2 = (c + s % 2) % 2
        return (replica, (x2 * NZ + (z + dz) % NZ) * 2 + c2)

    def at_y(dy, dl=0):
        return (((xlo + dl) % 2) * NY + (y + dy) % NY, expert)

    loads = [
        pltpu.make_async_copy(tok_h, tok.at[0], load_sem.at[0]),
        pltpu.make_async_copy(hid_h, hid, load_sem.at[1]),
        pltpu.make_async_copy(gate_h, w.at[:, :, pl.ds(0, 384)], load_sem.at[2]),
        pltpu.make_async_copy(up_h, w.at[:, :, pl.ds(384, 384)], load_sem.at[3]),
        pltpu.make_async_copy(inner_h, yr.at[y], load_sem.at[4]),
    ]
    for load in loads:
        load.start()

    barrier = pltpu.get_barrier_semaphore()
    peers = [at(dz) for dz in range(1, NZ)] + [at(0, s) for s in (1, 2, 3)]
    peers += [at_y(dy) for dy in range(1, NY)] + [at_y(0, 1)]
    for peer in peers:
        pl.semaphore_signal(barrier, inc=1, device_id=peer, device_id_type=MESH)
    pl.semaphore_wait(barrier, len(peers))

    def remote(src, dst, send, recv, device):
        return pltpu.make_async_remote_copy(
            src_ref=src, dst_ref=dst, send_sem=send, recv_sem=recv,
            device_id=device, device_id_type=MESH,
        )

    def token_copy(step, way, half):
        sign = 1 if way == 0 else -1
        rows = pl.ds(half * 64, 64)
        dst = POS[(sign * step) % NZ]
        src = tok_h.at[rows] if step == 1 else tok.at[POS[(sign * (step - 1)) % NZ], rows]
        return remote(
            src, tok.at[dst, rows], tok_s.at[dst, half], tok_r.at[dst, half], at(-sign)
        )

    def meta_copy(step, way):
        sign = 1 if way == 0 else -1
        dst = POS[(sign * step) % NZ]
        return remote(
            meta.at[POS[(sign * (step - 1)) % NZ]], meta.at[dst],
            meta_s.at[dst], meta_r.at[dst], at(-sign),
        )

    def ways(step, half):
        return (0, 1) if step < NZ // 2 else (half,)

    sent = []

    def go(copy):
        copy.start()
        sent.append(copy)
        return copy

    ring = {}
    for half in (0, 1):
        for way in ways(1, half):
            ring[1, way, half] = go(token_copy(1, way, half))
    gathers = [
        go(remote(inner_h, yr.at[y], y_s.at[dy], y_r.at[dy], at_y(dy))) for dy in range(1, NY)
    ]

    pick = onehot(iota((128, 1024), 1) // 8 == iota((128, 1024), 0))
    spread = jnp.dot(ids_ref[...].astype(F32).astype(BF16), pick, preferred_element_type=F32)
    mine = iota((8, 1024), 1) % 8 == iota((8, 1024), 0)
    ids = jnp.sum(jnp.where(mine, spread, 0.0), axis=0, keepdims=True)
    earlier = onehot(iota((512, 512), 0) // 8 < iota((512, 512), 1) // 8)
    experts = iota((96, 512), 0).astype(F32)
    slots = []
    for block in (0, 1):
        hits = experts == ids[:, block * 512 : (block + 1) * 512]
        before = jnp.dot(onehot(hits), earlier, preferred_element_type=F32)
        slots.append(
            jnp.sum(jnp.where(hits, before, 0.0), axis=0, keepdims=True) + float(SLOTS * block)
        )
    slot = jnp.concatenate(slots, axis=1)
    chip = jnp.floor(ids * 0.25)
    far_x = jnp.where(chip >= float(NZ), 1.0, 0.0)
    inside = ids - 4.0 * chip
    core = jnp.where(inside >= 2.0, 1.0, 0.0)
    local = inside - 2.0 * core
    dz = chip - float(NZ) * far_x - z.astype(F32)
    dz = jnp.where(dz < 0.0, dz + float(NZ), dz)
    rel = jnp.where(far_x == xhi.astype(F32), 0.0, 2.0) + jnp.where(core == c.astype(F32), 0.0, 1.0)
    lane = rel * 32.0 + local * 16.0 + slot
    order = jnp.zeros_like(dz)
    for q, distance in enumerate(FAR):
        order = order + jnp.where(dz == float(distance), float(q), 0.0)
    third_of = jnp.floor(order * 0.25)
    row = third_of * (4.0 * LINE) + rel * float(LINE) + (order - 4.0 * third_of) * float(PAIR)
    row = row + local * 14.0 + slot
    token = (iota((16, 1024), 1) // 8 + 1).astype(F32)
    lines = jnp.where(iota((16, 1024), 0).astype(F32) == dz, token, 0.0).astype(BF16)
    places = onehot(iota((128, 1024), 0).astype(F32) == lane)
    meta[0] = lax.dot_general(
        lines, places, (((1,), (1,)), ((), ())), preferred_element_type=F32
    )
    metas = {}
    for way in (0, 1):
        metas[1, way] = go(meta_copy(1, way))

    loads[1].wait()
    plane = {}
    rows_of = iota((4 * LINE, 1024), 0).astype(F32)
    for third in range(3):
        take = onehot(rows_of == row - float(4 * LINE * third))
        packed = jnp.dot(take, hid[...], preferred_element_type=F32).astype(BF16)
        hs[third] = packed
        for s in (1, 2, 3):
            piece = pl.ds(s * LINE, LINE)
            plane[third, s] = go(
                remote(
                    hs.at[third, piece], hq.at[third, piece],
                    hp_s.at[third, s], hp_r.at[third, s], at(0, s),
                )
            )
        hq[third, 0:LINE] = packed[0:LINE]

    rows_sent = {}

    def pick_rows(offset):
        p = POS[offset]
        line = (-offset) % NZ
        wanted = meta[p][line : line + 1, :]
        take = onehot((iota((128, 128), 0) + 1).astype(F32) == wanted)
        rows = lax.dot_general(
            take, tok[p], (((0,), (0,)), ((), ())), preferred_element_type=F32
        ).astype(BF16)
        for s in range(4):
            for e in range(2):
                at_row = (s * 2 + e) * ROWS
                xs[p, s, e] = rows[at_row : at_row + ROWS]
        for s in (1, 2, 3):
            rows_sent[p, s] = go(
                remote(xs.at[p, s], xr.at[p, s], x_s.at[p, s], x_r.at[p, s], at(0, s))
            )
        rows_sent[p, 0] = pltpu.make_async_copy(xs.at[p, 0], xr.at[p, 0], x_r.at[p, 0])
        rows_sent[p, 0].start()

    along = {}
    column = iota((1, 4 * LINE), 1).astype(F32)
    sender, receiver, rest = digits(column, LINE, PAIR)
    turned = onehot(
        iota((4 * LINE, 4 * LINE), 0).astype(F32) == receiver * LINE + sender * PAIR + rest
    )

    def turn(third):
        for s in (1, 2, 3):
            plane[third, s].wait_recv()
        lines = jnp.dot(turned, hq[third], preferred_element_type=F32).astype(BF16)
        hz[third] = lines
        for i in range(4):
            if FAR[4 * third + i] == 0:
                hr[0, 0:LINE] = lines[i * LINE : (i + 1) * LINE]

    def leave(q):
        p = POS[(-FAR[q]) % NZ]
        along[p] = go(
            remote(
                hz.at[q // 4, pl.ds(q % 4 * LINE, LINE)],
                hr.at[p // 4, pl.ds(p % 4 * LINE, LINE)],
                hz_s.at[p], hz_r.at[p], at(FAR[q]),
            )
        )

    outs = []

    def project(group):
        for p in range(4 * group, 4 * group + 4):
            rows_sent[p, 0].wait()
            for s in (1, 2, 3):
                rows_sent[p, s].wait_recv()
        for e in range(2):
            block = pl.ds(4 * group, 4)
            rows = xr[block, :, e].reshape(256, 1024)
            xt[e, :, 256 * group : 256 * group + 256] = rows.T
            gu[e, group] = jnp.dot(rows, w[e], preferred_element_type=F32)
            if group == FINISH[2]:
                out = pltpu.make_async_copy(
                    xt.at[e, :, pl.ds(256 * group, 256)], x_o.at[e], out_sem.at[0, e]
                )
                out.start()
                outs.append(out)

    loads[0].wait()
    pick_rows(0)
    for step in range(1, NZ // 2 + 1):
        for half in (0, 1):
            for way in ways(step, half):
                ring[step, way, half].wait_recv()
                if step < NZ // 2 and way in ways(step + 1, half):
                    ring[step + 1, way, half] = go(token_copy(step + 1, way, half))
            if half == 0:
                for way in ways(step, 0):
                    metas[step, way].wait_recv()
                    if step < NZ // 2 and way in ways(step + 1, 0):
                        metas[step + 1, way] = go(meta_copy(step + 1, way))
        for third in range(3):
            if min(LEAVE[4 * third : 4 * third + 4]) == step:
                turn(third)
        for q in range(NZ):
            if LEAVE[q] == step and FAR[q] != 0:
                leave(q)
        for offset in dict.fromkeys((step, NZ - step)):
            pick_rows(offset)
        if step == 3:
            loads[4].wait()
            for gather in gathers:
                gather.wait_recv()
            total = yr[0]
            for i in range(1, NY):
                total = total + yr[i]
            part[0] = total
            swap = go(remote(part.at[0], part.at[1], l_s, l_r, at_y(0, 1)))
        if step == 4:
            loads[2].wait()
            loads[3].wait()
            project(0)
        if step == 5:
            swap.wait_recv()
            sum_o[...] = part[0] + part[1]
        if step == 6:
            project(1)
    project(2)

    at_p, at_s, at_e, at_slot = digits(column, LINE, PAIR, 14)
    target = iota((256, 4 * LINE), 0).astype(F32)
    goal = (at_p * 4.0 + at_s) * float(ROWS) + at_slot
    spaced = [onehot((target == goal) & (at_e == float(e))) for e in range(2)]
    for group in FINISH:
        for p in range(4 * group, 4 * group + 4):
            if p in along:
                along[p].wait_recv()
        for e in range(2):
            cot = jnp.dot(spaced[e], hr[group], preferred_element_type=F32)
            gate = gu[e, group, :, 0:384]
            up = gu[e, group, :, 384:768]
            sig = jax.nn.sigmoid(gate)
            gd[e, group, :, 0:384] = (cot * up * sig * (1.0 + gate * (1.0 - sig))).astype(BF16)
            gd[e, group, :, 384:768] = (cot * gate * sig).astype(BF16)
            if group == FINISH[2]:
                out = pltpu.make_async_copy(gd.at[e, group], g_o.at[e], out_sem.at[1, e])
                out.start()
                outs.append(out)
                continue
            for m in range(4):
                rows = slice(256 * m, 256 * m + 256)
                grads = jnp.dot(
                    xt[e, rows, 256 * group : 256 * group + 256],
                    gd[e, group],
                    preferred_element_type=F32,
                )
                if group == FINISH[0]:
                    acc[e, rows] = grads
                else:
                    some[e, rows] = (acc[e, rows] + grads).astype(BF16)
            if group == FINISH[1]:
                out = pltpu.make_async_copy(some.at[e], some_o.at[e], out_sem.at[2, e])
                out.start()
                outs.append(out)
    for copy in sent:
        copy.wait_send()
    for out in outs:
        out.wait()


def grad_kernel(x_ref, g_ref, some_ref, sum_ref, outer_ref, mom_ref, gate_ref, up_ref, no_ref, nm_ref):
    grads = jnp.dot(x_ref[0], g_ref[0], preferred_element_type=F32)
    grads = (grads + some_ref[0].astype(F32)).astype(BF16)
    gate_ref[0] = grads[:, 0:384]
    up_ref[0] = grads[:, 384:768]
    delta = outer_ref[...] - sum_ref[...] / 16.0
    momentum = 0.9 * mom_ref[...] + delta
    nm_ref[...] = momentum
    no_ref[...] = outer_ref[...] - 0.7 * (delta + 0.9 * momentum)


def local(tokens, ids, hidden, gate_weight, up_weight, outer, momentum, inner):
    any_ = pl.BlockSpec(memory_space=pl.ANY)
    vmem = pl.BlockSpec(memory_space=pltpu.VMEM)
    dma = pltpu.SemaphoreType.DMA
    x_rows, g_rows, some, summed = pl.pallas_call(
        dispatch_kernel,
        out_shape=(
            jax.ShapeDtypeStruct((2, 1024, 256), BF16),
            jax.ShapeDtypeStruct((2, 256, 768), BF16),
            jax.ShapeDtypeStruct((2, 1024, 768), BF16),
            jax.ShapeDtypeStruct((8, 2048), F32),
        ),
        in_specs=[vmem, any_, any_, any_, any_, any_],
        out_specs=(any_, any_, any_, vmem),
        scratch_shapes=[
            pltpu.VMEM((NZ, 128, 1024), BF16),
            pltpu.VMEM((NZ, 16, 128), F32),
            pltpu.VMEM((NZ, 4, 2, ROWS, 1024), BF16),
            pltpu.VMEM((NZ, 4, 2, ROWS, 1024), BF16),
            pltpu.VMEM((2, 1024, 768), BF16),
            pltpu.VMEM((1024, 384), BF16),
            pltpu.VMEM((3, 4 * LINE, 384), BF16),
            pltpu.VMEM((3, 4 * LINE, 384), BF16),
            pltpu.VMEM((3, 4 * LINE, 384), BF16),
            pltpu.VMEM((3, 4 * LINE, 384), BF16),
            pltpu.VMEM((2, 1024, 768), BF16),
            pltpu.VMEM((2, 3, 256, 768), F32),
            pltpu.VMEM((2, 3, 256, 768), BF16),
            pltpu.VMEM((2, 1024, 768), F32),
            pltpu.VMEM((2, 1024, 768), BF16),
            pltpu.VMEM((NY, 8, 2048), F32),
            pltpu.VMEM((2, 8, 2048), F32),
            dma((5,)), dma((NZ, 2)), dma((NZ, 2)), dma((NZ,)), dma((NZ,)),
            dma((NZ, 4)), dma((NZ, 4)), dma((3, 4)), dma((3, 4)), dma((NZ,)), dma((NZ,)),
            dma((NY,)), dma((NY,)), dma, dma, dma((3, 2)),
        ],
        compiler_params=pltpu.CompilerParams(
            collective_id=0, has_side_effects=True, vmem_limit_bytes=60 << 20
        ),
        cost_estimate=pl.CostEstimate(
            flops=4_000_000_000, bytes_accessed=16_000_000, transcendentals=600_000
        ),
    )(ids[0].T, tokens[0], hidden[0].reshape(1024, 384), gate_weight, up_weight, inner[0])
    gate_grad, up_grad, new_outer, new_momentum = pl.pallas_call(
        grad_kernel,
        grid=(2, 2),
        out_shape=(
            jax.ShapeDtypeStruct((2, 1024, 384), BF16),
            jax.ShapeDtypeStruct((2, 1024, 384), BF16),
            jax.ShapeDtypeStruct((8, 2048), F32),
            jax.ShapeDtypeStruct((8, 2048), F32),
        ),
        in_specs=[
            pl.BlockSpec((1, 512, 256), lambda e, m: (e, m, 0)),
            pl.BlockSpec((1, 256, 768), lambda e, m: (e, 0, 0)),
            pl.BlockSpec((1, 512, 768), lambda e, m: (e, m, 0)),
            pl.BlockSpec((8, 2048), lambda e, m: (0, 0)),
            pl.BlockSpec((8, 2048), lambda e, m: (0, 0)),
            pl.BlockSpec((8, 2048), lambda e, m: (0, 0)),
        ],
        out_specs=(
            pl.BlockSpec((1, 512, 384), lambda e, m: (e, m, 0)),
            pl.BlockSpec((1, 512, 384), lambda e, m: (e, m, 0)),
            pl.BlockSpec((8, 2048), lambda e, m: (0, 0)),
            pl.BlockSpec((8, 2048), lambda e, m: (0, 0)),
        ),
        compiler_params=pltpu.CompilerParams(vmem_limit_bytes=60 << 20),
    )(x_rows, g_rows, some, summed, outer, momentum)
    return gate_grad[None], up_grad[None], new_outer, new_momentum


def solution(mesh):
    rows = P("replica", "expert", None)
    return jax.shard_map(
        local,
        mesh=mesh,
        in_specs=(
            rows,
            rows,
            P("replica", "expert", None, None),
            P("expert", None, None),
            P("expert", None, None),
            P("expert", None),
            P("expert", None),
            rows,
        ),
        out_specs=(
            P("replica", "expert", None, None),
            P("replica", "expert", None, None),
            P("expert", None),
            P("expert", None),
        ),
        check_vma=False,
    )
```

```python
import jax
import jax.numpy as jnp
from jax import lax
from jax.experimental import pallas as pl
from jax.experimental.pallas import tpu as pltpu
from jax.sharding import PartitionSpec as P

MESH = pl.DeviceIdType.MESH
NZ = 12
NY = 8
SLOTS = 7
ROWS = 16
ARRIVAL = [0, 1, 11, 2, 10, 3, 9, 4, 8, 5, 7, 6]
POS = {o: p for p, o in enumerate(ARRIVAL)}
FAR = [6, 5, 7, 4, 8, 3, 9, 2, 10, 1, 11, 0]
LEAVE = (4, 4, 5, 5, 5, 5, 5, 6, 6, 6, 6, 6)
FINISH = (2, 1, 0)
PAIR = 28
LINE = 4 * PAIR
PIECES = 2
TILES = 1
F32 = jnp.float32
BF16 = jnp.bfloat16


def iota(shape, dim):
    return lax.broadcasted_iota(jnp.int32, shape, dim)


def onehot(mask):
    return jnp.where(mask, 1.0, 0.0).astype(BF16)


def digits(value, *weights):
    out = []
    for weight in weights:
        digit = jnp.floor((value + 0.5) * (1.0 / weight))
        value = value - digit * weight
        out.append(digit)
    return (*out, value)


def dispatch_kernel(
    ids_ref, tok_h, hid_h, gate_h, up_h, inner_h,
    x_o, g_o, some_o, sum_o,
    tok, meta, xs, xr, xt, hid, hs, hq, hz, hr, w, gu, gd, acc, some, yr, part,
    load_sem, tok_s, tok_r, meta_s, meta_r, x_s, x_r, hp_s, hp_r, hz_s, hz_r,
    y_s, y_r, l_s, l_r, out_sem,
):
    replica = lax.axis_index("replica")
    expert = lax.axis_index("expert")
    xlo, y = replica // NY, replica % NY
    xhi, z, c = expert // (2 * NZ), (expert // 2) % NZ, expert % 2

    def at(dz=0, s=0):
        x2 = (xhi + s // 2) % 2
        c2 = (c + s % 2) % 2
        return (replica, (x2 * NZ + (z + dz) % NZ) * 2 + c2)

    def at_y(dy, dl=0):
        return (((xlo + dl) % 2) * NY + (y + dy) % NY, expert)

    loads = [
        pltpu.make_async_copy(tok_h, tok.at[0], load_sem.at[0]),
        pltpu.make_async_copy(hid_h, hid, load_sem.at[1]),
        pltpu.make_async_copy(gate_h, w.at[:, :, pl.ds(0, 384)], load_sem.at[2]),
        pltpu.make_async_copy(up_h, w.at[:, :, pl.ds(384, 384)], load_sem.at[3]),
        pltpu.make_async_copy(inner_h, yr.at[y], load_sem.at[4]),
    ]
    for load in loads:
        load.start()

    barrier = pltpu.get_barrier_semaphore()
    peers = [at(dz) for dz in range(1, NZ)] + [at(0, s) for s in (1, 2, 3)]
    peers += [at_y(dy) for dy in range(1, NY)] + [at_y(0, 1)]
    for peer in peers:
        pl.semaphore_signal(barrier, inc=1, device_id=peer, device_id_type=MESH)
    pl.semaphore_wait(barrier, len(peers))

    def remote(src, dst, send, recv, device):
        return pltpu.make_async_remote_copy(
            src_ref=src, dst_ref=dst, send_sem=send, recv_sem=recv,
            device_id=device, device_id_type=MESH,
        )

    def token_copy(step, way, piece_no):
        sign = 1 if way == 0 else -1
        rows = pl.ds(piece_no * (128 // PIECES), 128 // PIECES)
        dst = POS[(sign * step) % NZ]
        src = tok_h.at[rows] if step == 1 else tok.at[POS[(sign * (step - 1)) % NZ], rows]
        return remote(
            src, tok.at[dst, rows], tok_s.at[dst, piece_no], tok_r.at[dst, piece_no], at(-sign)
        )

    def meta_copy(step, way):
        sign = 1 if way == 0 else -1
        dst = POS[(sign * step) % NZ]
        return remote(
            meta.at[POS[(sign * (step - 1)) % NZ]], meta.at[dst],
            meta_s.at[dst], meta_r.at[dst], at(-sign),
        )

    def ways(step, piece_no):
        return (0, 1) if step < NZ // 2 else (piece_no // (PIECES // 2),)

    sent = []

    def go(copy):
        copy.start()
        sent.append(copy)
        return copy

    ring = {}
    for piece_no in range(PIECES):
        for way in ways(1, piece_no):
            ring[1, way, piece_no] = go(token_copy(1, way, piece_no))
    gathers = [
        go(remote(inner_h, yr.at[y], y_s.at[dy], y_r.at[dy], at_y(dy))) for dy in range(1, NY)
    ]

    pick = onehot(iota((128, 1024), 1) // 8 == iota((128, 1024), 0))
    spread = jnp.dot(ids_ref[...].astype(F32).astype(BF16), pick, preferred_element_type=F32)
    mine = iota((8, 1024), 1) % 8 == iota((8, 1024), 0)
    ids = jnp.sum(jnp.where(mine, spread, 0.0), axis=0, keepdims=True)
    earlier = onehot(iota((512, 512), 0) // 8 < iota((512, 512), 1) // 8)
    experts = iota((96, 512), 0).astype(F32)
    slots = []
    for block in (0, 1):
        hits = experts == ids[:, block * 512 : (block + 1) * 512]
        before = jnp.dot(onehot(hits), earlier, preferred_element_type=F32)
        slots.append(
            jnp.sum(jnp.where(hits, before, 0.0), axis=0, keepdims=True) + float(SLOTS * block)
        )
    slot = jnp.concatenate(slots, axis=1)
    chip = jnp.floor(ids * 0.25)
    far_x = jnp.where(chip >= float(NZ), 1.0, 0.0)
    inside = ids - 4.0 * chip
    core = jnp.where(inside >= 2.0, 1.0, 0.0)
    local = inside - 2.0 * core
    dz = chip - float(NZ) * far_x - z.astype(F32)
    dz = jnp.where(dz < 0.0, dz + float(NZ), dz)
    rel = jnp.where(far_x == xhi.astype(F32), 0.0, 2.0) + jnp.where(core == c.astype(F32), 0.0, 1.0)
    lane = rel * 32.0 + local * 16.0 + slot
    order = jnp.zeros_like(dz)
    for q, distance in enumerate(FAR):
        order = order + jnp.where(dz == float(distance), float(q), 0.0)
    third_of = jnp.floor(order * 0.25)
    row = third_of * (4.0 * LINE) + rel * float(LINE) + (order - 4.0 * third_of) * float(PAIR)
    row = row + local * 14.0 + slot
    token = (iota((16, 1024), 1) // 8 + 1).astype(F32)
    lines = jnp.where(iota((16, 1024), 0).astype(F32) == dz, token, 0.0).astype(BF16)
    places = onehot(iota((128, 1024), 0).astype(F32) == lane)
    meta[0] = lax.dot_general(
        lines, places, (((1,), (1,)), ((), ())), preferred_element_type=F32
    ).astype(BF16)
    metas = {}
    for way in (0, 1):
        metas[1, way] = go(meta_copy(1, way))

    loads[1].wait()
    plane = {}
    rows_of = iota((4 * LINE, 1024), 0).astype(F32)
    for third in range(3):
        take = onehot(rows_of == row - float(4 * LINE * third))
        packed = jnp.dot(take, hid[...], preferred_element_type=F32).astype(BF16)
        hs[third] = packed
        for s in (1, 2, 3):
            piece = pl.ds(s * LINE, LINE)
            plane[third, s] = go(
                remote(
                    hs.at[third, piece], hq.at[third, piece],
                    hp_s.at[third, s], hp_r.at[third, s], at(0, s),
                )
            )
        hq[third, 0:LINE] = packed[0:LINE]

    rows_sent = {}

    def pick_rows(offset):
        p = POS[offset]
        line = (-offset) % NZ
        wanted = meta[p].astype(F32)[line : line + 1, :]
        take = onehot((iota((128, 128), 0) + 1).astype(F32) == wanted)
        rows = lax.dot_general(
            take, tok[p], (((0,), (0,)), ((), ())), preferred_element_type=F32
        ).astype(BF16)
        for s in range(4):
            for e in range(2):
                at_row = (s * 2 + e) * ROWS
                xs[p, s, e] = rows[at_row : at_row + ROWS]
        for s in (1, 2, 3):
            rows_sent[p, s] = go(
                remote(xs.at[p, s], xr.at[p, s], x_s.at[p, s], x_r.at[p, s], at(0, s))
            )
        rows_sent[p, 0] = pltpu.make_async_copy(xs.at[p, 0], xr.at[p, 0], x_r.at[p, 0])
        rows_sent[p, 0].start()

    along = {}
    column = iota((1, 4 * LINE), 1).astype(F32)
    sender, receiver, rest = digits(column, LINE, PAIR)
    turned = onehot(
        iota((4 * LINE, 4 * LINE), 0).astype(F32) == receiver * LINE + sender * PAIR + rest
    )

    def turn(third):
        for s in (1, 2, 3):
            plane[third, s].wait_recv()
        lines = jnp.dot(turned, hq[third], preferred_element_type=F32).astype(BF16)
        hz[third] = lines
        for i in range(4):
            if FAR[4 * third + i] == 0:
                hr[0, 0:LINE] = lines[i * LINE : (i + 1) * LINE]

    def leave(q):
        p = POS[(-FAR[q]) % NZ]
        along[p] = go(
            remote(
                hz.at[q // 4, pl.ds(q % 4 * LINE, LINE)],
                hr.at[p // 4, pl.ds(p % 4 * LINE, LINE)],
                hz_s.at[p], hz_r.at[p], at(FAR[q]),
            )
        )

    outs = []

    def project(group):
        for p in range(4 * group, 4 * group + 4):
            rows_sent[p, 0].wait()
            for s in (1, 2, 3):
                rows_sent[p, s].wait_recv()
        for e in range(2):
            block = pl.ds(4 * group, 4)
            rows = xr[block, :, e].reshape(256, 1024)
            xt[e, :, 256 * group : 256 * group + 256] = rows.T
            gu[e, group] = jnp.dot(rows, w[e], preferred_element_type=F32)
            if group == FINISH[2]:
                out = pltpu.make_async_copy(
                    xt.at[e, :, pl.ds(256 * group, 256)], x_o.at[e], out_sem.at[0, e]
                )
                out.start()
                outs.append(out)

    loads[0].wait()
    pick_rows(0)
    for step in range(1, NZ // 2 + 1):
        for piece_no in range(PIECES):
            for way in ways(step, piece_no):
                ring[step, way, piece_no].wait_recv()
                if step < NZ // 2 and way in ways(step + 1, piece_no):
                    ring[step + 1, way, piece_no] = go(token_copy(step + 1, way, piece_no))
            if piece_no == 0:
                for way in ways(step, 0):
                    metas[step, way].wait_recv()
                    if step < NZ // 2 and way in ways(step + 1, 0):
                        metas[step + 1, way] = go(meta_copy(step + 1, way))
        for third in range(3):
            if min(LEAVE[4 * third : 4 * third + 4]) == step:
                turn(third)
        for q in range(NZ):
            if LEAVE[q] == step and FAR[q] != 0:
                leave(q)
        for offset in dict.fromkeys((step, NZ - step)):
            pick_rows(offset)
        if step == 3:
            loads[4].wait()
            for gather in gathers:
                gather.wait_recv()
            total = yr[0]
            for i in range(1, NY):
                total = total + yr[i]
            part[0] = total
            swap = go(remote(part.at[0], part.at[1], l_s, l_r, at_y(0, 1)))
        if step == 4:
            loads[2].wait()
            loads[3].wait()
            project(0)
        if step == 5:
            swap.wait_recv()
            sum_o[...] = part[0] + part[1]
        if step == 6:
            project(1)
    project(2)

    at_p, at_s, at_e, at_slot = digits(column, LINE, PAIR, 14)
    target = iota((256, 4 * LINE), 0).astype(F32)
    goal = (at_p * 4.0 + at_s) * float(ROWS) + at_slot
    spaced = [onehot((target == goal) & (at_e == float(e))) for e in range(2)]
    for group in FINISH:
        for p in range(4 * group, 4 * group + 4):
            if p in along:
                along[p].wait_recv()
        for e in range(2):
            cot = jnp.dot(spaced[e], hr[group], preferred_element_type=F32)
            gate = gu[e, group, :, 0:384]
            up = gu[e, group, :, 384:768]
            sig = jax.nn.sigmoid(gate)
            gd[e, group, :, 0:384] = (cot * up * sig * (1.0 + gate * (1.0 - sig))).astype(BF16)
            gd[e, group, :, 384:768] = (cot * gate * sig).astype(BF16)
            if group == FINISH[2]:
                out = pltpu.make_async_copy(gd.at[e, group], g_o.at[e], out_sem.at[1, e])
                out.start()
                outs.append(out)
                continue
            grads = jnp.dot(
                xt[e, :, 256 * group : 256 * group + 256],
                gd[e, group],
                preferred_element_type=F32,
            )
            if group == FINISH[0]:
                acc[e] = grads
            else:
                some[e] = (acc[e] + grads).astype(BF16)
            if group == FINISH[1]:
                out = pltpu.make_async_copy(some.at[e], some_o.at[e], out_sem.at[2, e])
                out.start()
                outs.append(out)
    for copy in sent:
        copy.wait_send()
    for out in outs:
        out.wait()


def grad_kernel(
    x_h, g_h, some_h, sum_h, outer_h, mom_h,
    gate_o, up_o, outer_o, mom_o,
    x, g, some, grads, steps, in_sem, g_sem, step_sem, out_sem,
):
    tile = 1024 // TILES
    small = [
        pltpu.make_async_copy(ref, steps.at[i], step_sem.at[i])
        for i, ref in enumerate((sum_h, outer_h, mom_h))
    ]
    loads, g_loads = {}, []
    for e in range(2):
        g_loads.append(pltpu.make_async_copy(g_h.at[e], g.at[e], g_sem.at[e]))
        g_loads[e].start()
        for m in range(TILES):
            rows = pl.ds(tile * m, tile)
            loads[e, m] = (
                pltpu.make_async_copy(x_h.at[e, rows], x.at[e, rows], in_sem.at[e, m, 0]),
                pltpu.make_async_copy(some_h.at[e, rows], some.at[e, rows], in_sem.at[e, m, 1]),
            )
            for load in loads[e, m]:
                load.start()
        if e == 0:
            for load in small:
                load.start()
    outs = []

    def out(src, dst, sem):
        outs.append(pltpu.make_async_copy(src, dst, sem))
        outs[-1].start()

    for e in range(2):
        g_loads[e].wait()
        for m in range(TILES):
            rows = pl.ds(tile * m, tile)
            for load in loads[e, m]:
                load.wait()
            total = jnp.dot(x[e, rows], g[e], preferred_element_type=F32)
            total = (total + some[e, rows].astype(F32)).astype(BF16)
            grads[0, e, rows] = total[:, 0:384]
            grads[1, e, rows] = total[:, 384:768]
            out(grads.at[0, e, rows], gate_o.at[e, rows], out_sem.at[e, m, 0])
            out(grads.at[1, e, rows], up_o.at[e, rows], out_sem.at[e, m, 1])
        if e == 0:
            for load in small:
                load.wait()
            delta = steps[1] - steps[0] / 16.0
            momentum = 0.9 * steps[2] + delta
            steps[3] = steps[1] - 0.7 * (delta + 0.9 * momentum)
            steps[4] = momentum
            out(steps.at[3], outer_o, step_sem.at[3])
            out(steps.at[4], mom_o, step_sem.at[4])
    for copy in outs:
        copy.wait()


def local(tokens, ids, hidden, gate_weight, up_weight, outer, momentum, inner):
    any_ = pl.BlockSpec(memory_space=pl.ANY)
    vmem = pl.BlockSpec(memory_space=pltpu.VMEM)
    dma = pltpu.SemaphoreType.DMA
    x_rows, g_rows, some, summed = pl.pallas_call(
        dispatch_kernel,
        out_shape=(
            jax.ShapeDtypeStruct((2, 1024, 256), BF16),
            jax.ShapeDtypeStruct((2, 256, 768), BF16),
            jax.ShapeDtypeStruct((2, 1024, 768), BF16),
            jax.ShapeDtypeStruct((8, 2048), F32),
        ),
        in_specs=[vmem, any_, any_, any_, any_, any_],
        out_specs=(any_, any_, any_, vmem),
        scratch_shapes=[
            pltpu.VMEM((NZ, 128, 1024), BF16),
            pltpu.VMEM((NZ, 16, 128), BF16),
            pltpu.VMEM((NZ, 4, 2, ROWS, 1024), BF16),
            pltpu.VMEM((NZ, 4, 2, ROWS, 1024), BF16),
            pltpu.VMEM((2, 1024, 768), BF16),
            pltpu.VMEM((1024, 384), BF16),
            pltpu.VMEM((3, 4 * LINE, 384), BF16),
            pltpu.VMEM((3, 4 * LINE, 384), BF16),
            pltpu.VMEM((3, 4 * LINE, 384), BF16),
            pltpu.VMEM((3, 4 * LINE, 384), BF16),
            pltpu.VMEM((2, 1024, 768), BF16),
            pltpu.VMEM((2, 3, 256, 768), F32),
            pltpu.VMEM((2, 3, 256, 768), BF16),
            pltpu.VMEM((2, 1024, 768), F32),
            pltpu.VMEM((2, 1024, 768), BF16),
            pltpu.VMEM((NY, 8, 2048), F32),
            pltpu.VMEM((2, 8, 2048), F32),
            dma((5,)), dma((NZ, PIECES)), dma((NZ, PIECES)), dma((NZ,)), dma((NZ,)),
            dma((NZ, 4)), dma((NZ, 4)), dma((3, 4)), dma((3, 4)), dma((NZ,)), dma((NZ,)),
            dma((NY,)), dma((NY,)), dma, dma, dma((3, 2)),
        ],
        compiler_params=pltpu.CompilerParams(
            collective_id=0, has_side_effects=True, vmem_limit_bytes=60 << 20
        ),
        cost_estimate=pl.CostEstimate(
            flops=4_000_000_000, bytes_accessed=16_000_000, transcendentals=600_000
        ),
    )(ids[0].T, tokens[0], hidden[0].reshape(1024, 384), gate_weight, up_weight, inner[0])
    gate_grad, up_grad, new_outer, new_momentum = pl.pallas_call(
        grad_kernel,
        out_shape=(
            jax.ShapeDtypeStruct((2, 1024, 384), BF16),
            jax.ShapeDtypeStruct((2, 1024, 384), BF16),
            jax.ShapeDtypeStruct((8, 2048), F32),
            jax.ShapeDtypeStruct((8, 2048), F32),
        ),
        in_specs=[any_] * 6,
        out_specs=(any_,) * 4,
        scratch_shapes=[
            pltpu.VMEM((2, 1024, 256), BF16),
            pltpu.VMEM((2, 256, 768), BF16),
            pltpu.VMEM((2, 1024, 768), BF16),
            pltpu.VMEM((2, 2, 1024, 384), BF16),
            pltpu.VMEM((5, 8, 2048), F32),
            dma((2, TILES, 2)), dma((2,)), dma((5,)), dma((2, TILES, 2)),
        ],
        compiler_params=pltpu.CompilerParams(vmem_limit_bytes=60 << 20),
    )(x_rows, g_rows, some, summed, outer, momentum)
    return gate_grad[None], up_grad[None], new_outer, new_momentum


def solution(mesh):
    rows = P("replica", "expert", None)
    return jax.shard_map(
        local,
        mesh=mesh,
        in_specs=(
            rows,
            rows,
            P("replica", "expert", None, None),
            P("expert", None, None),
            P("expert", None, None),
            P("expert", None),
            P("expert", None),
            rows,
        ),
        out_specs=(
            P("replica", "expert", None, None),
            P("replica", "expert", None, None),
            P("expert", None),
            P("expert", None),
        ),
        check_vma=False,
    )
```

```python
import jax
import jax.numpy as jnp
from jax import lax
from jax.experimental import pallas as pl
from jax.experimental.pallas import tpu as pltpu
from jax.sharding import PartitionSpec as P

MESH = pl.DeviceIdType.MESH
NZ = 12
NY = 8
SLOTS = 7
ROWS = 16
ARRIVAL = [0, 1, 11, 2, 10, 3, 9, 4, 8, 5, 7, 6]
POS = {o: p for p, o in enumerate(ARRIVAL)}
FAR = [6, 5, 7, 4, 8, 3, 9, 2, 10, 1, 11, 0]
LEAVE = (4, 4, 5, 5, 5, 5, 5, 6, 6, 6, 6, 6)
FINISH = (2, 1, 0)
PAIR = 28
LINE = 4 * PAIR
PIECES = 2
TILES = 1
F32 = jnp.float32
BF16 = jnp.bfloat16


def iota(shape, dim):
    return lax.broadcasted_iota(jnp.int32, shape, dim)


def onehot(mask):
    return jnp.where(mask, 1.0, 0.0).astype(BF16)


def digits(value, *weights):
    out = []
    for weight in weights:
        digit = jnp.floor((value + 0.5) * (1.0 / weight))
        value = value - digit * weight
        out.append(digit)
    return (*out, value)


def dispatch_kernel(
    ids_ref, tok_h, hid_h, gate_h, up_h, inner_h,
    x_o, g_o, some_o, sum_o,
    tok, meta, xs, xr, xt, hid, hs, hq, hz, hr, w, gu, gd, acc, some, yr, part,
    load_sem, tok_s, tok_r, meta_s, meta_r, x_s, x_r, hp_s, hp_r, hz_s, hz_r,
    y_s, y_r, l_s, l_r, out_sem,
):
    replica = lax.axis_index("replica")
    expert = lax.axis_index("expert")
    xlo, y = replica // NY, replica % NY
    xhi, z, c = expert // (2 * NZ), (expert // 2) % NZ, expert % 2

    def at(dz=0, s=0):
        x2 = (xhi + s // 2) % 2
        c2 = (c + s % 2) % 2
        return (replica, (x2 * NZ + (z + dz) % NZ) * 2 + c2)

    def at_y(dy, dl=0):
        return (((xlo + dl) % 2) * NY + (y + dy) % NY, expert)

    loads = [
        pltpu.make_async_copy(tok_h, tok.at[0], load_sem.at[0]),
        pltpu.make_async_copy(hid_h, hid, load_sem.at[1]),
        pltpu.make_async_copy(gate_h, w.at[:, :, pl.ds(0, 384)], load_sem.at[2]),
        pltpu.make_async_copy(up_h, w.at[:, :, pl.ds(384, 384)], load_sem.at[3]),
        pltpu.make_async_copy(inner_h, yr.at[y], load_sem.at[4]),
    ]
    for load in loads:
        load.start()

    barrier = pltpu.get_barrier_semaphore()
    peers = [at(dz) for dz in range(1, NZ)] + [at(0, s) for s in (1, 2, 3)]
    peers += [at_y(dy) for dy in range(1, NY)] + [at_y(0, 1)]
    for peer in peers:
        pl.semaphore_signal(barrier, inc=1, device_id=peer, device_id_type=MESH)
    pl.semaphore_wait(barrier, len(peers))

    def remote(src, dst, send, recv, device):
        return pltpu.make_async_remote_copy(
            src_ref=src, dst_ref=dst, send_sem=send, recv_sem=recv,
            device_id=device, device_id_type=MESH,
        )

    def token_copy(step, way, piece_no):
        sign = 1 if way == 0 else -1
        rows = pl.ds(piece_no * (128 // PIECES), 128 // PIECES)
        dst = POS[(sign * step) % NZ]
        src = tok_h.at[rows] if step == 1 else tok.at[POS[(sign * (step - 1)) % NZ], rows]
        return remote(
            src, tok.at[dst, rows], tok_s.at[dst, piece_no], tok_r.at[dst, piece_no], at(-sign)
        )

    def meta_copy(step, way):
        sign = 1 if way == 0 else -1
        dst = POS[(sign * step) % NZ]
        return remote(
            meta.at[POS[(sign * (step - 1)) % NZ]], meta.at[dst],
            meta_s.at[dst], meta_r.at[dst], at(-sign),
        )

    def ways(step, piece_no):
        return (0, 1) if step < NZ // 2 else (piece_no // (PIECES // 2),)

    sent = []

    def go(copy):
        copy.start()
        sent.append(copy)
        return copy

    ring = {}
    for piece_no in range(PIECES):
        for way in ways(1, piece_no):
            ring[1, way, piece_no] = go(token_copy(1, way, piece_no))
    gathers = [
        go(remote(inner_h, yr.at[y], y_s.at[dy], y_r.at[dy], at_y(dy))) for dy in range(1, NY)
    ]

    pick = onehot(iota((128, 1024), 1) // 8 == iota((128, 1024), 0))
    spread = jnp.dot(ids_ref[...].astype(F32).astype(BF16), pick, preferred_element_type=F32)
    mine = iota((8, 1024), 1) % 8 == iota((8, 1024), 0)
    ids = jnp.sum(jnp.where(mine, spread, 0.0), axis=0, keepdims=True)
    earlier = onehot(iota((512, 512), 0) // 8 < iota((512, 512), 1) // 8)
    experts = iota((96, 512), 0).astype(F32)
    slots = []
    for block in (0, 1):
        hits = experts == ids[:, block * 512 : (block + 1) * 512]
        before = jnp.dot(onehot(hits), earlier, preferred_element_type=F32)
        slots.append(
            jnp.sum(jnp.where(hits, before, 0.0), axis=0, keepdims=True) + float(SLOTS * block)
        )
    slot = jnp.concatenate(slots, axis=1)
    chip = jnp.floor(ids * 0.25)
    far_x = jnp.where(chip >= float(NZ), 1.0, 0.0)
    inside = ids - 4.0 * chip
    core = jnp.where(inside >= 2.0, 1.0, 0.0)
    local = inside - 2.0 * core
    dz = chip - float(NZ) * far_x - z.astype(F32)
    dz = jnp.where(dz < 0.0, dz + float(NZ), dz)
    rel = jnp.where(far_x == xhi.astype(F32), 0.0, 2.0) + jnp.where(core == c.astype(F32), 0.0, 1.0)
    lane = rel * 32.0 + local * 16.0 + slot
    order = jnp.zeros_like(dz)
    for q, distance in enumerate(FAR):
        order = order + jnp.where(dz == float(distance), float(q), 0.0)
    third_of = jnp.floor(order * 0.25)
    row = third_of * (4.0 * LINE) + rel * float(LINE) + (order - 4.0 * third_of) * float(PAIR)
    row = row + local * 14.0 + slot
    token = (iota((16, 1024), 1) // 8 + 1).astype(F32)
    lines = jnp.where(iota((16, 1024), 0).astype(F32) == dz, token, 0.0).astype(BF16)
    places = onehot(iota((128, 1024), 0).astype(F32) == lane)
    meta[0] = lax.dot_general(
        lines, places, (((1,), (1,)), ((), ())), preferred_element_type=F32
    ).astype(BF16)
    metas = {}
    for way in (0, 1):
        metas[1, way] = go(meta_copy(1, way))

    loads[1].wait()
    plane = {}
    rows_of = iota((4 * LINE, 1024), 0).astype(F32)
    for third in range(3):
        take = onehot(rows_of == row - float(4 * LINE * third))
        packed = jnp.dot(take, hid[...], preferred_element_type=F32).astype(BF16)
        hs[third] = packed
        for s in (1, 2, 3):
            piece = pl.ds(s * LINE, LINE)
            plane[third, s] = go(
                remote(
                    hs.at[third, piece], hq.at[third, piece],
                    hp_s.at[third, s], hp_r.at[third, s], at(0, s),
                )
            )
        hq[third, 0:LINE] = packed[0:LINE]

    rows_sent = {}

    def pick_rows(offset):
        p = POS[offset]
        line = (-offset) % NZ
        wanted = meta[p].astype(F32)[line : line + 1, :]
        take = onehot((iota((128, 128), 0) + 1).astype(F32) == wanted)
        rows = lax.dot_general(
            take, tok[p], (((0,), (0,)), ((), ())), preferred_element_type=F32
        ).astype(BF16)
        for s in range(4):
            for e in range(2):
                at_row = (s * 2 + e) * ROWS
                xs[p, s, e] = rows[at_row : at_row + ROWS]
        for s in (1, 2, 3):
            rows_sent[p, s] = go(
                remote(xs.at[p, s], xr.at[p, s], x_s.at[p, s], x_r.at[p, s], at(0, s))
            )
        rows_sent[p, 0] = pltpu.make_async_copy(xs.at[p, 0], xr.at[p, 0], x_r.at[p, 0])
        rows_sent[p, 0].start()

    along = {}
    column = iota((1, 4 * LINE), 1).astype(F32)
    sender, receiver, rest = digits(column, LINE, PAIR)
    turned = onehot(
        iota((4 * LINE, 4 * LINE), 0).astype(F32) == receiver * LINE + sender * PAIR + rest
    )

    def turn(third):
        for s in (1, 2, 3):
            plane[third, s].wait_recv()
        lines = jnp.dot(turned, hq[third], preferred_element_type=F32).astype(BF16)
        hz[third] = lines
        for i in range(4):
            if FAR[4 * third + i] == 0:
                hr[0, 0:LINE] = lines[i * LINE : (i + 1) * LINE]

    def leave(q):
        p = POS[(-FAR[q]) % NZ]
        along[p] = go(
            remote(
                hz.at[q // 4, pl.ds(q % 4 * LINE, LINE)],
                hr.at[p // 4, pl.ds(p % 4 * LINE, LINE)],
                hz_s.at[p], hz_r.at[p], at(FAR[q]),
            )
        )

    outs = []

    def project(group):
        for p in range(4 * group, 4 * group + 4):
            rows_sent[p, 0].wait()
            for s in (1, 2, 3):
                rows_sent[p, s].wait_recv()
        for e in range(2):
            block = pl.ds(4 * group, 4)
            rows = xr[block, :, e].reshape(256, 1024)
            xt[e, :, 256 * group : 256 * group + 256] = rows.T
            gu[e, group] = jnp.dot(rows, w[e], preferred_element_type=F32)
            if group == FINISH[2]:
                out = pltpu.make_async_copy(
                    xt.at[e, :, pl.ds(256 * group, 256)], x_o.at[e], out_sem.at[0, e]
                )
                out.start()
                outs.append(out)

    loads[0].wait()
    pick_rows(0)
    for step in range(1, NZ // 2 + 1):
        for piece_no in range(PIECES):
            for way in ways(step, piece_no):
                ring[step, way, piece_no].wait_recv()
                if step < NZ // 2 and way in ways(step + 1, piece_no):
                    ring[step + 1, way, piece_no] = go(token_copy(step + 1, way, piece_no))
            if piece_no == 0:
                for way in ways(step, 0):
                    metas[step, way].wait_recv()
                    if step < NZ // 2 and way in ways(step + 1, 0):
                        metas[step + 1, way] = go(meta_copy(step + 1, way))
        for third in range(3):
            if min(LEAVE[4 * third : 4 * third + 4]) == step:
                turn(third)
        for q in range(NZ):
            if LEAVE[q] == step and FAR[q] != 0:
                leave(q)
        for offset in dict.fromkeys((step, NZ - step)):
            pick_rows(offset)
        if step == 3:
            loads[4].wait()
            for gather in gathers:
                gather.wait_recv()
            total = yr[0]
            for i in range(1, NY):
                total = total + yr[i]
            part[0] = total
            swap = go(remote(part.at[0], part.at[1], l_s, l_r, at_y(0, 1)))
        if step == 4:
            loads[2].wait()
            loads[3].wait()
            project(0)
        if step == 5:
            swap.wait_recv()
            sum_o[...] = part[0] + part[1]
        if step == 6:
            project(1)
    project(2)

    at_p, at_s, at_e, at_slot = digits(column, LINE, PAIR, 14)
    target = iota((256, 4 * LINE), 0).astype(F32)
    goal = (at_p * 4.0 + at_s) * float(ROWS) + at_slot
    spaced = [onehot((target == goal) & (at_e == float(e))) for e in range(2)]
    late = list(along.values())
    for copy in sent:
        if not any(copy is other for other in late):
            copy.wait_send()
    for group in FINISH:
        for p in range(4 * group, 4 * group + 4):
            if p in along:
                along[p].wait_recv()
        for e in range(2):
            cot = jnp.dot(spaced[e], hr[group], preferred_element_type=F32)
            gate = gu[e, group, :, 0:384]
            up = gu[e, group, :, 384:768]
            sig = jax.nn.sigmoid(gate)
            gd[e, group, :, 0:384] = (cot * up * sig * (1.0 + gate * (1.0 - sig))).astype(BF16)
            gd[e, group, :, 384:768] = (cot * gate * sig).astype(BF16)
            if group == FINISH[2]:
                out = pltpu.make_async_copy(gd.at[e, group], g_o.at[e], out_sem.at[1, e])
                out.start()
                outs.append(out)
                continue
            grads = jnp.dot(
                xt[e, :, 256 * group : 256 * group + 256],
                gd[e, group],
                preferred_element_type=F32,
            )
            if group == FINISH[0]:
                acc[e] = grads
            else:
                some[e] = (acc[e] + grads).astype(BF16)
            if group == FINISH[1]:
                out = pltpu.make_async_copy(some.at[e], some_o.at[e], out_sem.at[2, e])
                out.start()
                outs.append(out)
    for copy in late:
        copy.wait_send()
    for out in outs:
        out.wait()


def grad_kernel(
    x_h, g_h, some_h, sum_h, outer_h, mom_h,
    gate_o, up_o, outer_o, mom_o,
    x, g, some, grads, steps, in_sem, g_sem, step_sem, out_sem,
):
    tile = 1024 // TILES
    small = [
        pltpu.make_async_copy(ref, steps.at[i], step_sem.at[i])
        for i, ref in enumerate((sum_h, outer_h, mom_h))
    ]
    loads, g_loads = {}, []
    for e in range(2):
        g_loads.append(pltpu.make_async_copy(g_h.at[e], g.at[e], g_sem.at[e]))
        g_loads[e].start()
        for m in range(TILES):
            rows = pl.ds(tile * m, tile)
            loads[e, m] = (
                pltpu.make_async_copy(x_h.at[e, rows], x.at[e, rows], in_sem.at[e, m, 0]),
                pltpu.make_async_copy(some_h.at[e, rows], some.at[e, rows], in_sem.at[e, m, 1]),
            )
            for load in loads[e, m]:
                load.start()
        if e == 0:
            for load in small:
                load.start()
    outs = []

    def out(src, dst, sem):
        outs.append(pltpu.make_async_copy(src, dst, sem))
        outs[-1].start()

    for e in range(2):
        g_loads[e].wait()
        for m in range(TILES):
            rows = pl.ds(tile * m, tile)
            for load in loads[e, m]:
                load.wait()
            total = jnp.dot(x[e, rows], g[e], preferred_element_type=F32)
            total = (total + some[e, rows].astype(F32)).astype(BF16)
            grads[0, e, rows] = total[:, 0:384]
            grads[1, e, rows] = total[:, 384:768]
            out(grads.at[0, e, rows], gate_o.at[e, rows], out_sem.at[e, m, 0])
            out(grads.at[1, e, rows], up_o.at[e, rows], out_sem.at[e, m, 1])
        if e == 0:
            for load in small:
                load.wait()
            delta = steps[1] - steps[0] / 16.0
            momentum = 0.9 * steps[2] + delta
            steps[3] = steps[1] - 0.7 * (delta + 0.9 * momentum)
            steps[4] = momentum
            out(steps.at[3], outer_o, step_sem.at[3])
            out(steps.at[4], mom_o, step_sem.at[4])
    for copy in outs:
        copy.wait()


def local(tokens, ids, hidden, gate_weight, up_weight, outer, momentum, inner):
    any_ = pl.BlockSpec(memory_space=pl.ANY)
    vmem = pl.BlockSpec(memory_space=pltpu.VMEM)
    dma = pltpu.SemaphoreType.DMA
    x_rows, g_rows, some, summed = pl.pallas_call(
        dispatch_kernel,
        out_shape=(
            jax.ShapeDtypeStruct((2, 1024, 256), BF16),
            jax.ShapeDtypeStruct((2, 256, 768), BF16),
            jax.ShapeDtypeStruct((2, 1024, 768), BF16),
            jax.ShapeDtypeStruct((8, 2048), F32),
        ),
        in_specs=[vmem, any_, any_, any_, any_, any_],
        out_specs=(any_, any_, any_, vmem),
        scratch_shapes=[
            pltpu.VMEM((NZ, 128, 1024), BF16),
            pltpu.VMEM((NZ, 16, 128), BF16),
            pltpu.VMEM((NZ, 4, 2, ROWS, 1024), BF16),
            pltpu.VMEM((NZ, 4, 2, ROWS, 1024), BF16),
            pltpu.VMEM((2, 1024, 768), BF16),
            pltpu.VMEM((1024, 384), BF16),
            pltpu.VMEM((3, 4 * LINE, 384), BF16),
            pltpu.VMEM((3, 4 * LINE, 384), BF16),
            pltpu.VMEM((3, 4 * LINE, 384), BF16),
            pltpu.VMEM((3, 4 * LINE, 384), BF16),
            pltpu.VMEM((2, 1024, 768), BF16),
            pltpu.VMEM((2, 3, 256, 768), F32),
            pltpu.VMEM((2, 3, 256, 768), BF16),
            pltpu.VMEM((2, 1024, 768), F32),
            pltpu.VMEM((2, 1024, 768), BF16),
            pltpu.VMEM((NY, 8, 2048), F32),
            pltpu.VMEM((2, 8, 2048), F32),
            dma((5,)), dma((NZ, PIECES)), dma((NZ, PIECES)), dma((NZ,)), dma((NZ,)),
            dma((NZ, 4)), dma((NZ, 4)), dma((3, 4)), dma((3, 4)), dma((NZ,)), dma((NZ,)),
            dma((NY,)), dma((NY,)), dma, dma, dma((3, 2)),
        ],
        compiler_params=pltpu.CompilerParams(
            collective_id=0, has_side_effects=True, vmem_limit_bytes=60 << 20
        ),
        cost_estimate=pl.CostEstimate(
            flops=4_000_000_000, bytes_accessed=16_000_000, transcendentals=600_000
        ),
    )(ids[0].T, tokens[0], hidden[0].reshape(1024, 384), gate_weight, up_weight, inner[0])
    gate_grad, up_grad, new_outer, new_momentum = pl.pallas_call(
        grad_kernel,
        out_shape=(
            jax.ShapeDtypeStruct((2, 1024, 384), BF16),
            jax.ShapeDtypeStruct((2, 1024, 384), BF16),
            jax.ShapeDtypeStruct((8, 2048), F32),
            jax.ShapeDtypeStruct((8, 2048), F32),
        ),
        in_specs=[any_] * 6,
        out_specs=(any_,) * 4,
        scratch_shapes=[
            pltpu.VMEM((2, 1024, 256), BF16),
            pltpu.VMEM((2, 256, 768), BF16),
            pltpu.VMEM((2, 1024, 768), BF16),
            pltpu.VMEM((2, 2, 1024, 384), BF16),
            pltpu.VMEM((5, 8, 2048), F32),
            dma((2, TILES, 2)), dma((2,)), dma((5,)), dma((2, TILES, 2)),
        ],
        compiler_params=pltpu.CompilerParams(vmem_limit_bytes=60 << 20),
    )(x_rows, g_rows, some, summed, outer, momentum)
    return gate_grad[None], up_grad[None], new_outer, new_momentum


def solution(mesh):
    rows = P("replica", "expert", None)
    return jax.shard_map(
        local,
        mesh=mesh,
        in_specs=(
            rows,
            rows,
            P("replica", "expert", None, None),
            P("expert", None, None),
            P("expert", None, None),
            P("expert", None),
            P("expert", None),
            rows,
        ),
        out_specs=(
            P("replica", "expert", None, None),
            P("replica", "expert", None, None),
            P("expert", None),
            P("expert", None),
        ),
        check_vma=False,
    )
```

```python
import jax
import jax.numpy as jnp
from jax import lax
from jax.experimental import pallas as pl
from jax.experimental.pallas import tpu as pltpu
from jax.sharding import PartitionSpec as P

MESH = pl.DeviceIdType.MESH
NZ = 12
NY = 8
SLOTS = 7
ROWS = 16
ARRIVAL = [0, 1, 11, 2, 10, 3, 9, 4, 8, 5, 7, 6]
POS = {o: p for p, o in enumerate(ARRIVAL)}
FAR = [6, 5, 7, 4, 8, 3, 9, 2, 10, 1, 11, 0]
LEAVE = (4, 4, 4, 4, 5, 5, 5, 5, 5, 5, 5, 5)
FINISH = (2, 1, 0)
PAIR = 28
LINE = 4 * PAIR
PIECES = 2
TILES = 1
F32 = jnp.float32
BF16 = jnp.bfloat16


def iota(shape, dim):
    return lax.broadcasted_iota(jnp.int32, shape, dim)


def onehot(mask):
    return jnp.where(mask, 1.0, 0.0).astype(BF16)


def digits(value, *weights):
    out = []
    for weight in weights:
        digit = jnp.floor((value + 0.5) * (1.0 / weight))
        value = value - digit * weight
        out.append(digit)
    return (*out, value)


def dispatch_kernel(
    ids_ref, tok_h, hid_h, gate_h, up_h, inner_h,
    x_o, g_o, some_o, sum_o,
    tok, meta, xs, xr, xt, hid, hs, hq, hz, hr, w, gu, gd, acc, some, yr, part,
    load_sem, tok_s, tok_r, meta_s, meta_r, x_s, x_r, hp_s, hp_r, hz_s, hz_r,
    y_s, y_r, l_s, l_r, out_sem,
):
    replica = lax.axis_index("replica")
    expert = lax.axis_index("expert")
    xlo, y = replica // NY, replica % NY
    xhi, z, c = expert // (2 * NZ), (expert // 2) % NZ, expert % 2

    def at(dz=0, s=0):
        x2 = (xhi + s // 2) % 2
        c2 = (c + s % 2) % 2
        return (replica, (x2 * NZ + (z + dz) % NZ) * 2 + c2)

    def at_y(dy, dl=0):
        return (((xlo + dl) % 2) * NY + (y + dy) % NY, expert)

    loads = [
        pltpu.make_async_copy(tok_h, tok.at[0], load_sem.at[0]),
        pltpu.make_async_copy(hid_h, hid, load_sem.at[1]),
        pltpu.make_async_copy(gate_h, w.at[:, :, pl.ds(0, 384)], load_sem.at[2]),
        pltpu.make_async_copy(up_h, w.at[:, :, pl.ds(384, 384)], load_sem.at[3]),
        pltpu.make_async_copy(inner_h, yr.at[y], load_sem.at[4]),
    ]
    for load in loads:
        load.start()

    barrier = pltpu.get_barrier_semaphore()
    peers = [at(dz) for dz in range(1, NZ)] + [at(0, s) for s in (1, 2, 3)]
    peers += [at_y(dy) for dy in range(1, NY)] + [at_y(0, 1)]
    for peer in peers:
        pl.semaphore_signal(barrier, inc=1, device_id=peer, device_id_type=MESH)
    pl.semaphore_wait(barrier, len(peers))

    def remote(src, dst, send, recv, device):
        return pltpu.make_async_remote_copy(
            src_ref=src, dst_ref=dst, send_sem=send, recv_sem=recv,
            device_id=device, device_id_type=MESH,
        )

    def token_copy(step, way, piece_no):
        sign = 1 if way == 0 else -1
        rows = pl.ds(piece_no * (128 // PIECES), 128 // PIECES)
        dst = POS[(sign * step) % NZ]
        src = tok_h.at[rows] if step == 1 else tok.at[POS[(sign * (step - 1)) % NZ], rows]
        return remote(
            src, tok.at[dst, rows], tok_s.at[dst, piece_no], tok_r.at[dst, piece_no], at(-sign)
        )

    def meta_copy(step, way):
        sign = 1 if way == 0 else -1
        dst = POS[(sign * step) % NZ]
        return remote(
            meta.at[POS[(sign * (step - 1)) % NZ]], meta.at[dst],
            meta_s.at[dst], meta_r.at[dst], at(-sign),
        )

    def ways(step, piece_no):
        return (0, 1) if step < NZ // 2 else (piece_no // (PIECES // 2),)

    sent = []

    def go(copy):
        copy.start()
        sent.append(copy)
        return copy

    ring = {}
    for piece_no in range(PIECES):
        for way in ways(1, piece_no):
            ring[1, way, piece_no] = go(token_copy(1, way, piece_no))
    gathers = [
        go(remote(inner_h, yr.at[y], y_s.at[dy], y_r.at[dy], at_y(dy))) for dy in range(1, NY)
    ]

    pick = onehot(iota((128, 1024), 1) // 8 == iota((128, 1024), 0))
    spread = jnp.dot(ids_ref[...].astype(F32).astype(BF16), pick, preferred_element_type=F32)
    mine = iota((8, 1024), 1) % 8 == iota((8, 1024), 0)
    ids = jnp.sum(jnp.where(mine, spread, 0.0), axis=0, keepdims=True)
    earlier = onehot(iota((512, 512), 0) // 8 < iota((512, 512), 1) // 8)
    experts = iota((96, 512), 0).astype(F32)
    slots = []
    for block in (0, 1):
        hits = experts == ids[:, block * 512 : (block + 1) * 512]
        before = jnp.dot(onehot(hits), earlier, preferred_element_type=F32)
        slots.append(
            jnp.sum(jnp.where(hits, before, 0.0), axis=0, keepdims=True) + float(SLOTS * block)
        )
    slot = jnp.concatenate(slots, axis=1)
    chip = jnp.floor(ids * 0.25)
    far_x = jnp.where(chip >= float(NZ), 1.0, 0.0)
    inside = ids - 4.0 * chip
    core = jnp.where(inside >= 2.0, 1.0, 0.0)
    local = inside - 2.0 * core
    dz = chip - float(NZ) * far_x - z.astype(F32)
    dz = jnp.where(dz < 0.0, dz + float(NZ), dz)
    rel = jnp.where(far_x == xhi.astype(F32), 0.0, 2.0) + jnp.where(core == c.astype(F32), 0.0, 1.0)
    lane = rel * 32.0 + local * 16.0 + slot
    order = jnp.zeros_like(dz)
    for q, distance in enumerate(FAR):
        order = order + jnp.where(dz == float(distance), float(q), 0.0)
    third_of = jnp.floor(order * 0.25)
    row = third_of * (4.0 * LINE) + rel * float(LINE) + (order - 4.0 * third_of) * float(PAIR)
    row = row + local * 14.0 + slot
    token = (iota((16, 1024), 1) // 8 + 1).astype(F32)
    lines = jnp.where(iota((16, 1024), 0).astype(F32) == dz, token, 0.0).astype(BF16)
    places = onehot(iota((128, 1024), 0).astype(F32) == lane)
    meta[0] = lax.dot_general(
        lines, places, (((1,), (1,)), ((), ())), preferred_element_type=F32
    ).astype(BF16)
    metas = {}
    for way in (0, 1):
        metas[1, way] = go(meta_copy(1, way))

    loads[1].wait()
    plane = {}
    rows_of = iota((4 * LINE, 1024), 0).astype(F32)
    for third in range(3):
        take = onehot(rows_of == row - float(4 * LINE * third))
        packed = jnp.dot(take, hid[...], preferred_element_type=F32).astype(BF16)
        hs[third] = packed
        for s in (1, 2, 3):
            piece = pl.ds(s * LINE, LINE)
            plane[third, s] = go(
                remote(
                    hs.at[third, piece], hq.at[third, piece],
                    hp_s.at[third, s], hp_r.at[third, s], at(0, s),
                )
            )
        hq[third, 0:LINE] = packed[0:LINE]

    rows_sent = {}

    def pick_rows(offset):
        p = POS[offset]
        line = (-offset) % NZ
        wanted = meta[p].astype(F32)[line : line + 1, :]
        take = onehot((iota((128, 128), 0) + 1).astype(F32) == wanted)
        rows = lax.dot_general(
            take, tok[p], (((0,), (0,)), ((), ())), preferred_element_type=F32
        ).astype(BF16)
        for s in range(4):
            for e in range(2):
                at_row = (s * 2 + e) * ROWS
                xs[p, s, e] = rows[at_row : at_row + ROWS]
        for s in (1, 2, 3):
            rows_sent[p, s] = go(
                remote(xs.at[p, s], xr.at[p, s], x_s.at[p, s], x_r.at[p, s], at(0, s))
            )
        rows_sent[p, 0] = pltpu.make_async_copy(xs.at[p, 0], xr.at[p, 0], x_r.at[p, 0])
        rows_sent[p, 0].start()

    along = {}
    column = iota((1, 4 * LINE), 1).astype(F32)
    sender, receiver, rest = digits(column, LINE, PAIR)
    turned = onehot(
        iota((4 * LINE, 4 * LINE), 0).astype(F32) == receiver * LINE + sender * PAIR + rest
    )

    def turn(third):
        for s in (1, 2, 3):
            plane[third, s].wait_recv()
        lines = jnp.dot(turned, hq[third], preferred_element_type=F32).astype(BF16)
        hz[third] = lines
        for i in range(4):
            if FAR[4 * third + i] == 0:
                hr[0, 0:LINE] = lines[i * LINE : (i + 1) * LINE]

    def leave(q):
        p = POS[(-FAR[q]) % NZ]
        along[p] = go(
            remote(
                hz.at[q // 4, pl.ds(q % 4 * LINE, LINE)],
                hr.at[p // 4, pl.ds(p % 4 * LINE, LINE)],
                hz_s.at[p], hz_r.at[p], at(FAR[q]),
            )
        )

    outs = []

    def project(group):
        for p in range(4 * group, 4 * group + 4):
            rows_sent[p, 0].wait()
            for s in (1, 2, 3):
                rows_sent[p, s].wait_recv()
        for e in range(2):
            block = pl.ds(4 * group, 4)
            rows = xr[block, :, e].reshape(256, 1024)
            xt[e, :, 256 * group : 256 * group + 256] = rows.T
            gu[e, group] = jnp.dot(rows, w[e], preferred_element_type=F32)
            if group == FINISH[2]:
                out = pltpu.make_async_copy(
                    xt.at[e, :, pl.ds(256 * group, 256)], x_o.at[e], out_sem.at[0, e]
                )
                out.start()
                outs.append(out)

    loads[0].wait()
    pick_rows(0)
    for step in range(1, NZ // 2 + 1):
        for piece_no in range(PIECES):
            for way in ways(step, piece_no):
                ring[step, way, piece_no].wait_recv()
                if step < NZ // 2 and way in ways(step + 1, piece_no):
                    ring[step + 1, way, piece_no] = go(token_copy(step + 1, way, piece_no))
            if piece_no == 0:
                for way in ways(step, 0):
                    metas[step, way].wait_recv()
                    if step < NZ // 2 and way in ways(step + 1, 0):
                        metas[step + 1, way] = go(meta_copy(step + 1, way))
        for third in range(3):
            if min(LEAVE[4 * third : 4 * third + 4]) == step:
                turn(third)
        for q in range(NZ):
            if LEAVE[q] == step and FAR[q] != 0:
                leave(q)
        for offset in dict.fromkeys((step, NZ - step)):
            pick_rows(offset)
        if step == 3:
            loads[4].wait()
            for gather in gathers:
                gather.wait_recv()
            total = yr[0]
            for i in range(1, NY):
                total = total + yr[i]
            part[0] = total
            swap = go(remote(part.at[0], part.at[1], l_s, l_r, at_y(0, 1)))
        if step == 4:
            loads[2].wait()
            loads[3].wait()
            project(0)
        if step == 5:
            swap.wait_recv()
            sum_o[...] = part[0] + part[1]
        if step == 6:
            project(1)
    project(2)

    at_p, at_s, at_e, at_slot = digits(column, LINE, PAIR, 14)
    target = iota((256, 4 * LINE), 0).astype(F32)
    goal = (at_p * 4.0 + at_s) * float(ROWS) + at_slot
    spaced = [onehot((target == goal) & (at_e == float(e))) for e in range(2)]
    for group in FINISH:
        for p in range(4 * group, 4 * group + 4):
            if p in along:
                along[p].wait_recv()
        for e in range(2):
            cot = jnp.dot(spaced[e], hr[group], preferred_element_type=F32)
            gate = gu[e, group, :, 0:384]
            up = gu[e, group, :, 384:768]
            sig = jax.nn.sigmoid(gate)
            gd[e, group, :, 0:384] = (cot * up * sig * (1.0 + gate * (1.0 - sig))).astype(BF16)
            gd[e, group, :, 384:768] = (cot * gate * sig).astype(BF16)
            if group == FINISH[2]:
                out = pltpu.make_async_copy(gd.at[e, group], g_o.at[e], out_sem.at[1, e])
                out.start()
                outs.append(out)
                continue
            grads = jnp.dot(
                xt[e, :, 256 * group : 256 * group + 256],
                gd[e, group],
                preferred_element_type=F32,
            )
            if group == FINISH[0]:
                acc[e] = grads
            else:
                some[e] = (acc[e] + grads).astype(BF16)
            if group == FINISH[1]:
                out = pltpu.make_async_copy(some.at[e], some_o.at[e], out_sem.at[2, e])
                out.start()
                outs.append(out)
    for copy in sent:
        copy.wait_send()
    for out in outs:
        out.wait()


def grad_kernel(
    x_h, g_h, some_h, sum_h, outer_h, mom_h,
    gate_o, up_o, outer_o, mom_o,
    x, g, some, grads, steps, in_sem, g_sem, step_sem, out_sem,
):
    tile = 1024 // TILES
    small = [
        pltpu.make_async_copy(ref, steps.at[i], step_sem.at[i])
        for i, ref in enumerate((sum_h, outer_h, mom_h))
    ]
    loads, g_loads = {}, []
    for e in range(2):
        g_loads.append(pltpu.make_async_copy(g_h.at[e], g.at[e], g_sem.at[e]))
        g_loads[e].start()
        for m in range(TILES):
            rows = pl.ds(tile * m, tile)
            loads[e, m] = (
                pltpu.make_async_copy(x_h.at[e, rows], x.at[e, rows], in_sem.at[e, m, 0]),
                pltpu.make_async_copy(some_h.at[e, rows], some.at[e, rows], in_sem.at[e, m, 1]),
            )
            for load in loads[e, m]:
                load.start()
        if e == 0:
            for load in small:
                load.start()
    outs = []

    def out(src, dst, sem):
        outs.append(pltpu.make_async_copy(src, dst, sem))
        outs[-1].start()

    for e in range(2):
        g_loads[e].wait()
        for m in range(TILES):
            rows = pl.ds(tile * m, tile)
            for load in loads[e, m]:
                load.wait()
            total = jnp.dot(x[e, rows], g[e], preferred_element_type=F32)
            total = (total + some[e, rows].astype(F32)).astype(BF16)
            grads[0, e, rows] = total[:, 0:384]
            grads[1, e, rows] = total[:, 384:768]
            out(grads.at[0, e, rows], gate_o.at[e, rows], out_sem.at[e, m, 0])
            out(grads.at[1, e, rows], up_o.at[e, rows], out_sem.at[e, m, 1])
        if e == 0:
            for load in small:
                load.wait()
            delta = steps[1] - steps[0] / 16.0
            momentum = 0.9 * steps[2] + delta
            steps[3] = steps[1] - 0.7 * (delta + 0.9 * momentum)
            steps[4] = momentum
            out(steps.at[3], outer_o, step_sem.at[3])
            out(steps.at[4], mom_o, step_sem.at[4])
    for copy in outs:
        copy.wait()


def local(tokens, ids, hidden, gate_weight, up_weight, outer, momentum, inner):
    any_ = pl.BlockSpec(memory_space=pl.ANY)
    vmem = pl.BlockSpec(memory_space=pltpu.VMEM)
    dma = pltpu.SemaphoreType.DMA
    x_rows, g_rows, some, summed = pl.pallas_call(
        dispatch_kernel,
        out_shape=(
            jax.ShapeDtypeStruct((2, 1024, 256), BF16),
            jax.ShapeDtypeStruct((2, 256, 768), BF16),
            jax.ShapeDtypeStruct((2, 1024, 768), BF16),
            jax.ShapeDtypeStruct((8, 2048), F32),
        ),
        in_specs=[vmem, any_, any_, any_, any_, any_],
        out_specs=(any_, any_, any_, vmem),
        scratch_shapes=[
            pltpu.VMEM((NZ, 128, 1024), BF16),
            pltpu.VMEM((NZ, 16, 128), BF16),
            pltpu.VMEM((NZ, 4, 2, ROWS, 1024), BF16),
            pltpu.VMEM((NZ, 4, 2, ROWS, 1024), BF16),
            pltpu.VMEM((2, 1024, 768), BF16),
            pltpu.VMEM((1024, 384), BF16),
            pltpu.VMEM((3, 4 * LINE, 384), BF16),
            pltpu.VMEM((3, 4 * LINE, 384), BF16),
            pltpu.VMEM((3, 4 * LINE, 384), BF16),
            pltpu.VMEM((3, 4 * LINE, 384), BF16),
            pltpu.VMEM((2, 1024, 768), BF16),
            pltpu.VMEM((2, 3, 256, 768), F32),
            pltpu.VMEM((2, 3, 256, 768), BF16),
            pltpu.VMEM((2, 1024, 768), F32),
            pltpu.VMEM((2, 1024, 768), BF16),
            pltpu.VMEM((NY, 8, 2048), F32),
            pltpu.VMEM((2, 8, 2048), F32),
            dma((5,)), dma((NZ, PIECES)), dma((NZ, PIECES)), dma((NZ,)), dma((NZ,)),
            dma((NZ, 4)), dma((NZ, 4)), dma((3, 4)), dma((3, 4)), dma((NZ,)), dma((NZ,)),
            dma((NY,)), dma((NY,)), dma, dma, dma((3, 2)),
        ],
        compiler_params=pltpu.CompilerParams(
            collective_id=0, has_side_effects=True, vmem_limit_bytes=60 << 20
        ),
        cost_estimate=pl.CostEstimate(
            flops=4_000_000_000, bytes_accessed=16_000_000, transcendentals=600_000
        ),
    )(ids[0].T, tokens[0], hidden[0].reshape(1024, 384), gate_weight, up_weight, inner[0])
    gate_grad, up_grad, new_outer, new_momentum = pl.pallas_call(
        grad_kernel,
        out_shape=(
            jax.ShapeDtypeStruct((2, 1024, 384), BF16),
            jax.ShapeDtypeStruct((2, 1024, 384), BF16),
            jax.ShapeDtypeStruct((8, 2048), F32),
            jax.ShapeDtypeStruct((8, 2048), F32),
        ),
        in_specs=[any_] * 6,
        out_specs=(any_,) * 4,
        scratch_shapes=[
            pltpu.VMEM((2, 1024, 256), BF16),
            pltpu.VMEM((2, 256, 768), BF16),
            pltpu.VMEM((2, 1024, 768), BF16),
            pltpu.VMEM((2, 2, 1024, 384), BF16),
            pltpu.VMEM((5, 8, 2048), F32),
            dma((2, TILES, 2)), dma((2,)), dma((5,)), dma((2, TILES, 2)),
        ],
        compiler_params=pltpu.CompilerParams(vmem_limit_bytes=60 << 20),
    )(x_rows, g_rows, some, summed, outer, momentum)
    return gate_grad[None], up_grad[None], new_outer, new_momentum


def solution(mesh):
    rows = P("replica", "expert", None)
    return jax.shard_map(
        local,
        mesh=mesh,
        in_specs=(
            rows,
            rows,
            P("replica", "expert", None, None),
            P("expert", None, None),
            P("expert", None, None),
            P("expert", None),
            P("expert", None),
            rows,
        ),
        out_specs=(
            P("replica", "expert", None, None),
            P("replica", "expert", None, None),
            P("expert", None),
            P("expert", None),
        ),
        check_vma=False,
    )
```
